256 devices in a mesh: prow: 8 (over x, y_lo), pcol: 32 (over y_hi, z, core).
Axes of the slice: x: 4, y: 4 (y_hi: 2, y_lo: 2; y = y_hi * 2 + y_lo), z: 8, core: 2. Of those that a mesh axis runs over, the one named last changes fastest.
Arguments:
- anc_inverse: bfloat16 [12, 2048, 3, 8192], P(None, 'prow', None, 'pcol'), may hold values from -0.0390625 to 0.0390625
- panel: bfloat16 [3, 12, 8, 256, 512], P(None, None, 'prow', 'pcol'), may hold values from -1.1953125 to 1.1953125
- tile_mask: int32 [3, 96], replicated, may hold values 0 or 1
- diag_inverse: float32 [3, 512, 512], P(None, ('prow', 'pcol')), may hold values from -6 to 6
Outputs:
- block_column: bfloat16 [3, 12, 8, 256, 512], P(None, None, 'prow', 'pcol')
- diag_block: float32 [3, 512, 512], P(None, ('prow', 'pcol'))
The draws below stay inside these ranges and needn't reach their ends.
All inputs are finite; a program needn't handle non-finite values.
Results may differ from the reference program's by a relative error of at most 0.0017.
Values may be sent and summed in bfloat16 or wider, within the bound.
A program may use at most 128 MiB of HBM per device.

```python
import jax
import jax.numpy as jnp
from jax import lax

TILE = 256
W = 512
S = 3
CT = 3
TILES = 96
RT = 12
N_PROW = 8
N_PCOL = 32


def set_ends(entries, own_key, low, high):
    place = [jax.random.randint(jax.random.fold_in(own_key, axis), (), 0, length) for axis, length in enumerate(entries.shape)]
    main_axis = entries.shape.index(max(entries.shape))
    neighbour = place[:main_axis] + [(place[main_axis] + 1) % entries.shape[main_axis]] + place[main_axis + 1:]
    return entries.at[tuple(place)].set(low).at[tuple(neighbour)].set(high)


def steps_of(stream_key, extent, pieces, least, high):
    level = 1.0
    for position, shards_of in pieces:
        draws = jax.random.uniform(jax.random.fold_in(jax.random.fold_in(stream_key, 6), position), (shards_of,), jnp.float32, least / len(pieces), high / len(pieces))
        level = level * jnp.repeat(jnp.exp(draws), extent[position] // shards_of).reshape((-1,) + (1,) * (len(extent) - 1 - position))
    return level


def noise(own_key, extent, deviation, limit, pieces=(), held_as=jnp.bfloat16):
    loudness = steps_of(own_key, extent, pieces, -0.22, 0.18) if pieces else 1.0
    drawn = jax.random.normal(own_key, extent, jnp.float32) * deviation * loudness
    return jnp.minimum(jnp.maximum(drawn, -limit), limit).astype(held_as)


def setup_inputs(seed: int = 0) -> dict:
    splits = jax.random.split(jax.random.key(seed), 5)
    return {
        "anc_inverse": noise(splits[0], (RT, N_PROW * TILE, CT, N_PCOL * TILE), (TILES * TILE) ** -0.5, 0.0390625, ((1, 8), (3, 32))),
        "panel": noise(splits[1], (S, RT, N_PROW, TILE, W), 0.15, 1.1953125, ((2, 8), (3, 32))),
        "tile_mask": set_ends((jax.random.randint(splits[2], (S, TILES), 0, 16) < 13).astype(jnp.int32), jax.random.fold_in(splits[2], 1), 0, 1),
        "diag_inverse": noise(splits[3], (S, W, W), 1.0, 6.0, ((1, 256),), jnp.float32),
    }


def reference(anc_inverse, panel, tile_mask, diag_inverse):
    order = anc_inverse.shape[0] * anc_inverse.shape[1]
    full = anc_inverse.reshape(order, order)
    panel_flat = panel.reshape(S, order, W)
    keeps = jnp.repeat(tile_mask, TILE, axis=1).astype(jnp.bfloat16)

    def single(items):
        lpanel, keep, dinv = items
        masked = lpanel * keep[:, None]
        product = jnp.dot(full, masked, preferred_element_type=jnp.float32)
        column = (-product * keep[:, None].astype(jnp.float32)).astype(jnp.bfloat16)
        diag = dinv - jnp.dot(masked.T, column, preferred_element_type=jnp.float32)
        return column, diag

    columns, diags = lax.map(single, (panel_flat, keeps, diag_inverse))
    return columns.reshape(panel.shape), diags
```

```python
import functools

import jax
import jax.numpy as jnp
from jax import lax
from jax.experimental import pallas as pl
from jax.experimental.pallas import tpu as pltpu
from jax.sharding import PartitionSpec as P

MESH = pl.DeviceIdType.MESH
F32 = jnp.float32
BF16 = jnp.bfloat16
I16 = jnp.int16
SUB = 8
LEVELS = 32000.0
LAG = 2


def kernel(
    NP, NCOL, mask_ref, anc_ref, panel_ref, dinv_ref, col_ref, diag_ref,
    mfull, mf, sib, mpair, lbuf, cbuf, sbuf, rbuf, ysb, yrb, colp, perm, mpt,
    dsend, drecv, esend, erecv,
    m_l, m_s, m_r, a0_s, a0_r, a1_s, a1_r, a2_s, a2_r, a3_s, a3_r,
    r_s, r_r, y_s, y_r, c_s, c_r, d_s, d_r, e_s, e_r,
):
    SETS, RT, _, W = panel_ref.shape
    CT = anc_ref.shape[1]
    TILE = anc_ref.shape[2]
    HALF = RT // 2
    NC = NCOL // 2
    Z = NC // 2
    NH = NCOL // NP
    NT = 2 * NP
    LC = W // 4
    WH = W // 2
    TH = HALF // 2
    ROWS = HALF * 16
    NG = ROWS // SUB
    HOPS = Z - 1

    p = lax.axis_index("prow")
    q = lax.axis_index("pcol")
    core = lax.rem(q, 2)
    chip = q // 2
    z = lax.rem(chip, Z)
    yh = chip // Z
    sibling = (p, q + 1 - 2 * core)
    t_me = p * 2 + yh

    def at_chip(row, y, depth):
        return (row, (y * Z + depth) * 2 + core)

    def plane(step):
        other = lax.rem(t_me + step, NT)
        return at_chip(other // 2, lax.rem(other, 2), z)

    up = at_chip(p, yh, lax.rem(z + 1, Z))
    down = at_chip(p, yh, lax.rem(z + Z - 1, Z))
    y_mate = at_chip(p, 1 - yh, z)

    a1_row = lax.rem(chip, NP)
    a1_core = chip // NP

    def a1_target(h2):
        h = 2 * core + h2
        return (a1_row, 2 * (h * (NP // 2) + p // 2) + a1_core)

    def a1_is_me(h2):
        row, column = a1_target(h2)
        return jnp.logical_and(row == p, column == q)

    def a1_source(half):
        return (2 * lax.rem(chip, NP // 2) + half, 2 * (core * NP + p) + yh)

    def signal(where):
        pl.semaphore_signal(barrier, inc=1, device_id=where, device_id_type=MESH)

    barrier = pltpu.get_barrier_semaphore()
    signal(sibling)

    @pl.loop(1, NT)
    def _(step):
        signal(plane(step))

    @pl.loop(1, Z)
    def _(step):
        signal(at_chip(p, yh, lax.rem(z + step, Z)))

    expected = 1 + (NT - 1) + (Z - 1)
    for e in range(2):
        me = a1_is_me(e)
        row, column = a1_source(e)
        from_me = jnp.logical_and(row == p, column == q)

        @pl.when(jnp.logical_not(me))
        def _():
            signal(a1_target(e))

        @pl.when(jnp.logical_not(from_me))
        def _():
            signal((row, column))

        expected = expected + jnp.where(me, 0, 1) + jnp.where(from_me, 0, 1)

    def copy(src, dst, send, recv, where):
        return pltpu.make_async_remote_copy(
            src_ref=src, dst_ref=dst, send_sem=send, recv_sem=recv,
            device_id=where, device_id_type=MESH,
        )

    def lanes(half, b):
        return pl.ds(pl.multiple_of((half * CT + b) * TILE, TILE), TILE)

    def m_local(b):
        return pltpu.make_async_copy(
            anc_ref.at[pl.ds(core * HALF, HALF), b], mfull.at[:, :, lanes(core, b)], m_l.at[b])

    def m_swap(b):
        return copy(
            anc_ref.at[pl.ds((1 - core) * HALF, HALF), b], mfull.at[:, :, lanes(core, b)],
            m_s.at[b], m_r.at[b], sibling)

    for b in range(CT):
        m_local(b).start()

    def keep(s, a):
        return mask_ref[s, a * NP + p].astype(F32)

    @pl.loop(0, SETS)
    def _(s):
        @pl.loop(0, RT)
        def _(a):
            mf[s, a] = panel_ref[s, a].astype(F32) * keep(s, a)

    rows = lax.broadcasted_iota(jnp.int32, (WH, W), 0)
    columns = lax.broadcasted_iota(jnp.int32, (WH, W), 1)
    hit = columns == (rows >> 1) * 4 + 2 * core + (rows & 1)
    perm[...] = jnp.where(hit, 1.0, 0.0).astype(BF16)

    pl.semaphore_wait(barrier, expected)

    def a0(s):
        return copy(mf.at[s], sib.at[s], a0_s.at[s], a0_r.at[s], sibling)

    for s in range(SETS):
        a0(s).start()
    for b in range(CT):
        m_swap(b).start()

    def l_slice(s, index):
        return lbuf.at[s, :, pl.ds(pl.multiple_of(16 * index, 16), 16), :]

    def a1_dst(s):
        return lbuf.at[s, pl.ds(lax.rem(p, 2) * CT, CT), pl.ds(pl.multiple_of(16 * chip, 16), 16), :]

    def a1(s, h2):
        return copy(mpair.at[s, :, 2 * core + h2], a1_dst(s), a1_s.at[s, h2], a1_r.at[s], a1_target(h2))

    def a1_local(s, h2):
        return pltpu.make_async_copy(mpair.at[s, :, 2 * core + h2], a1_dst(s), a1_r.at[s])

    mine = core * NP + p

    def a1_wait(s):
        copy(l_slice(s, mine), l_slice(s, mine), a1_s.at[s, 0], a1_r.at[s], sibling).wait_recv()

    @pl.loop(0, SETS)
    def _(s):
        a0(s).wait_recv()
        own = mf[s]
        other = sib[s]
        low = jnp.where(core == 0, own, other)
        high = jnp.where(core == 0, other, own)
        both = jnp.concatenate([low, high], axis=1)
        mpair[s] = both.astype(BF16).reshape(CT, NH, 16, W)
        for h2 in range(2):
            me = a1_is_me(h2)

            @pl.when(me)
            def _():
                a1_local(s, h2).start()

            @pl.when(jnp.logical_not(me))
            def _():
                a1(s, h2).start()

        mpt[s] = lax.dot_general(
            perm[...], mpair[s].reshape(RT * 16, W), (((1,), (1,)), ((), ())),
            preferred_element_type=F32).astype(BF16)

    def a2(s, step):
        where = (lax.rem(p + step, NP), q)
        return copy(l_slice(s, mine), l_slice(s, mine), a2_s.at[s, step], a2_r.at[s, step], where)

    def a2_sibling(s):
        return copy(l_slice(s, mine), l_slice(s, mine), a2_s.at[s, 0], a2_r.at[s, 0], sibling)

    def a3(s, step):
        index = core * NP + lax.rem(p + NP - step, NP)
        return copy(l_slice(s, index), l_slice(s, index), a3_s.at[s, step], a3_r.at[s, step], sibling)

    def spread(s):
        a1_wait(s)

        @pl.loop(1, NP)
        def _(step):
            a2(s, step).start()

        a2_sibling(s).start()

    def piece(s, d, depth, j):
        return (s, pl.ds(d * TH, TH), slice(None), depth, slice(None), pl.ds(j * LC, LC))

    def y_piece(s, y, j):
        return (s, slice(None), y, z, slice(None), pl.ds(j * LC, LC))

    def pack(index, dst):
        top = jnp.zeros((SUB, LC), F32)
        for j in range(4):
            v = cbuf[index(j)].reshape(NG, SUB, LC)
            top = jnp.maximum(top, jnp.max(jnp.abs(v), axis=0))
        power = jnp.minimum(jnp.maximum(jnp.ceil(jnp.log2(top)), -100.0), 100.0)
        factor = jnp.exp2(-power) * LEVELS
        for j in range(4):
            v = cbuf[index(j)].reshape(NG, SUB, LC) * factor[None]
            whole = jnp.round(v).astype(jnp.int32).astype(I16)
            dst[pl.ds(j * ROWS, ROWS), :] = whole.reshape(ROWS, LC)
        power = power.astype(jnp.int32)
        dst[pl.ds(4 * ROWS, 16), :] = jnp.concatenate([power, power], axis=0).astype(I16)

    def scale_of(src):
        power = src[pl.ds(4 * ROWS, 16), :].astype(jnp.int32).astype(F32)[:SUB]
        return jnp.exp2(power) * (1.0 / LEVELS)

    def unpack(src, scale, j):
        v = src[pl.ds(j * ROWS, ROWS), :].astype(jnp.int32).astype(F32)
        return v.reshape(NG, SUB, LC) * scale[None]

    def hop_chunk(d, k):
        return lax.rem(jnp.where(d == 0, z + 2 * Z - 1 - k, z + 1 + k), Z)

    def hop(s, d, k):
        where = (p, jnp.where(d == 0, up[1], down[1]))
        return copy(sbuf.at[s, d, k], rbuf.at[s, d, k], r_s.at[s, d, k], r_r.at[s, d, k], where)

    def ring_step(s, d, k):
        depth = hop_chunk(d, k)

        @pl.when(k > 0)
        def _():
            hop(s, d, k - 1).wait_recv()
            src = rbuf.at[s, d, k - 1]
            scale = scale_of(src)
            for j in range(4):
                index = piece(s, d, depth, j)
                shape = (TH, 2, 16, LC)
                cbuf[index] = cbuf[index] + unpack(src, scale, j).reshape(shape)

        @pl.when(k < HOPS)
        def _():
            pack(lambda j: piece(s, d, depth, j), sbuf.at[s, d, k])
            hop(s, d, k).start()

    def y_copy(s):
        return copy(ysb.at[s], yrb.at[s], y_s.at[s], y_r.at[s], y_mate)

    def c_copy(s):
        return copy(colp.at[s, core], colp.at[s, core], c_s.at[s], c_r.at[s], sibling)

    def arrive(s):
        @pl.loop(1, NP)
        def _(step):
            a2(s, step).wait_recv()
            a3(s, step).start()

        @pl.when(s + 1 < SETS)
        def _():
            spread(s + 1)

        a2_sibling(s).wait_recv()

        @pl.loop(1, NP)
        def _(step):
            a3(s, step).wait_recv()

        @pl.when(s == 0)
        def _():
            for b in range(CT):
                m_local(b).wait()
                m_swap(b).wait_recv()

        @pl.loop(0, HALF)
        def _(a):
            product = jnp.dot(
                mfull[a], lbuf[s].reshape(2 * CT * TILE, W), preferred_element_type=F32)
            cbuf[s, a] = product.reshape(2, Z, 16, W)

    def y_arrive(s):
        y_copy(s).wait_recv()
        src = yrb.at[s]
        scale = scale_of(src)
        for j in range(4):
            total = cbuf[y_piece(s, yh, j)] + unpack(src, scale, j).reshape(HALF, 16, LC)
            for a in range(HALF):
                image = -total[a] * keep(s, core * HALF + a)
                colp[s, core, a, :, pl.ds(j * LC, LC)] = image.astype(BF16)
        c_copy(s).start()

    def d_copy(s, step):
        other = lax.rem(t_me + step, NT)
        return copy(dsend.at[s, other], drecv.at[s, step], d_s.at[s, step], d_r.at[s, step], plane(step))

    def c_arrive(s):
        c_copy(s).wait_recv()
        dsend[s] = jnp.dot(
            mpt[s], colp[s].reshape(RT * 16, W), preferred_element_type=F32).reshape(NT, 2 * Z, W)

        @pl.loop(1, NT)
        def _(step):
            d_copy(s, step).start()

        both = colp[s].reshape(RT, 16, W).astype(F32)
        picked = jnp.where(core == 0, both[:, :SUB], both[:, SUB:])
        col_ref[s] = picked.astype(BF16)

    def d_arrive(s):
        @pl.loop(1, NT)
        def _(step):
            d_copy(s, step).wait_recv()

        total = dsend[s, t_me]
        for step in range(1, NT):
            total = total + drecv[s, step]
        for depth in range(Z):
            esend[depth, s] = total[2 * depth : 2 * depth + 2]

    spread(0)

    @pl.loop(0, (SETS - 1) * LAG + HOPS + 4)
    def _(t):
        @pl.loop(0, SETS)
        def _(s):
            k = t - s * LAG

            @pl.when(k == 0)
            def _():
                arrive(s)

            @pl.when(jnp.logical_and(k >= 0, k <= HOPS))
            def _():
                @pl.loop(0, 2)
                def _(d):
                    ring_step(s, d, k)

            @pl.when(k == HOPS)
            def _():
                pack(lambda j: y_piece(s, 1 - yh, j), ysb.at[s])
                y_copy(s).start()

            @pl.when(k == HOPS + 1)
            def _():
                y_arrive(s)

            @pl.when(k == HOPS + 2)
            def _():
                c_arrive(s)

            @pl.when(k == HOPS + 3)
            def _():
                d_arrive(s)

    def e_copy(step):
        other = lax.rem(z + step, Z)
        return copy(esend.at[other], erecv.at[step], e_s.at[step], e_r.at[step], at_chip(p, yh, other))

    @pl.loop(1, Z)
    def _(step):
        e_copy(step).start()

    @pl.loop(1, Z)
    def _(step):
        e_copy(step).wait_recv()

    total = esend[z]
    for step in range(1, Z):
        total = total + erecv[step]
    diag_ref[...] = dinv_ref[...] - total

    for b in range(CT):
        m_swap(b).wait_send()

    @pl.loop(0, SETS)
    def _(s):
        a0(s).wait_send()
        for h2 in range(2):
            @pl.when(jnp.logical_not(a1_is_me(h2)))
            def _():
                a1(s, h2).wait_send()

        a2_sibling(s).wait_send()

        @pl.loop(1, NP)
        def _(step):
            a2(s, step).wait_send()
            a3(s, step).wait_send()

        @pl.loop(0, HOPS)
        def _(k):
            hop(s, 0, k).wait_send()
            hop(s, 1, k).wait_send()

        y_copy(s).wait_send()
        c_copy(s).wait_send()

        @pl.loop(1, NT)
        def _(step):
            d_copy(s, step).wait_send()

    @pl.loop(1, Z)
    def _(step):
        e_copy(step).wait_send()


def body(anc_inverse, panel, tile_mask, diag_inverse):
    n_row = lax.axis_size("prow")
    n_col = lax.axis_size("pcol")
    sets, rt, _, sub, w = panel.shape
    _, tile, ct, _ = anc_inverse.shape
    anc = jnp.transpose(anc_inverse, (0, 2, 1, 3))
    slim = panel.reshape(sets, rt, sub, w)
    half, nz, nt, nh = rt // 2, n_col // 4, 2 * n_row, n_col // n_row
    hops = nz - 1
    lc = w // 4
    message = 4 * half * 16 + 16
    dma = pltpu.SemaphoreType.DMA
    vmem = pl.BlockSpec(memory_space=pltpu.VMEM)
    scratch = [
        pltpu.VMEM((half, tile, 2 * ct * tile), BF16),
        pltpu.VMEM((sets, rt, sub, w), F32),
        pltpu.VMEM((sets, rt, sub, w), F32),
        pltpu.VMEM((sets, ct, nh, 16, w), BF16),
        pltpu.VMEM((sets, 2 * ct, tile, w), BF16),
        pltpu.VMEM((sets, half, 2, nz, 16, w), F32),
        pltpu.VMEM((sets, 2, hops, message, lc), I16),
        pltpu.VMEM((sets, 2, hops, message, lc), I16),
        pltpu.VMEM((sets, message, lc), I16),
        pltpu.VMEM((sets, message, lc), I16),
        pltpu.VMEM((sets, 2, half, 16, w), BF16),
        pltpu.VMEM((w // 2, w), BF16),
        pltpu.VMEM((sets, w // 2, rt * 16), BF16),
        pltpu.VMEM((sets, nt, 2 * nz, w), F32),
        pltpu.VMEM((sets, nt, 2 * nz, w), F32),
        pltpu.VMEM((nz, sets, 2, w), F32),
        pltpu.VMEM((nz, sets, 2, w), F32),
        dma((ct,)), dma((ct,)), dma((ct,)),
        dma((sets,)), dma((sets,)),
        dma((sets, 2)), dma((sets,)),
        dma((sets, n_row)), dma((sets, n_row)),
        dma((sets, n_row)), dma((sets, n_row)),
        dma((sets, 2, hops)), dma((sets, 2, hops)),
        dma((sets,)), dma((sets,)),
        dma((sets,)), dma((sets,)),
        dma((sets, nt)), dma((sets, nt)),
        dma((nz,)), dma((nz,)),
    ]
    column, diag = pl.pallas_call(
        functools.partial(kernel, n_row, n_col),
        out_shape=(
            jax.ShapeDtypeStruct((sets, rt, sub, w), BF16),
            jax.ShapeDtypeStruct(diag_inverse.shape, F32),
        ),
        in_specs=[
            pl.BlockSpec(memory_space=pltpu.SMEM),
            pl.BlockSpec(memory_space=pl.ANY),
            vmem,
            vmem,
        ],
        out_specs=(vmem, vmem),
        scratch_shapes=scratch,
        compiler_params=pltpu.CompilerParams(
            collective_id=0, has_side_effects=True, vmem_limit_bytes=56 * 1024 * 1024
        ),
        name="selected_inverse",
    )(tile_mask, anc, slim, diag_inverse)
    return column.reshape(panel.shape), diag


def solution(mesh):
    in_specs = (
        P(None, "prow", None, "pcol"),
        P(None, None, "prow", "pcol", None),
        P(),
        P(None, ("prow", "pcol"), None),
    )
    out_specs = (P(None, None, "prow", "pcol", None), P(None, ("prow", "pcol"), None))
    return jax.shard_map(body, mesh=mesh, in_specs=in_specs, out_specs=out_specs, check_vma=False)
```

```python
import functools

import jax
import jax.numpy as jnp
from jax import lax
from jax.experimental import pallas as pl
from jax.experimental.pallas import tpu as pltpu
from jax.sharding import PartitionSpec as P

MESH = pl.DeviceIdType.MESH
F32 = jnp.float32
BF16 = jnp.bfloat16
I16 = jnp.int16
SUB = 8
LEVELS = 32000.0
PARTS = 2
LAG = 1
AHEAD = 2


def kernel(
    NP, NCOL, mask_ref, anc_ref, panel_ref, dinv_ref, col_ref, diag_ref,
    mfull, mf, sib, mpair, lbuf, cbuf, sbuf, rbuf, ysb, yrb, colp, perm, mpt,
    dsend, drecv, fsend, frecv, esend, erecv,
    m_l, m_s, m_r, a0_s, a0_r, a1_s, a1_r, l_s, a2_r, a3_r,
    r_s, r_r, y_s, y_r, c_s, c_r, d_s, d_r, f_s, f_r, e_s, e_r,
):
    SETS, RT, _, W = panel_ref.shape
    CT = anc_ref.shape[1]
    TILE = anc_ref.shape[-1]
    HALF = RT // 2
    NC = NCOL // 2
    Z = NC // 2
    NH = NCOL // NP
    WP = W // PARTS
    COUNT = SETS * PARTS
    LC = WP // 2
    WH = W // 2
    X = NP // 2
    NU = 4
    LONG = Z // 2
    SHORT = Z - 1 - LONG

    p = lax.axis_index("prow")
    q = lax.axis_index("pcol")
    core = lax.rem(q, 2)
    chip = q // 2
    z = lax.rem(chip, Z)
    yh = chip // Z
    sibling = (p, q + 1 - 2 * core)

    def at_chip(row, y, depth):
        return (row, (y * Z + depth) * 2 + core)

    u_me = lax.rem(p, 2) * 2 + yh

    def x_line(step):
        return at_chip(2 * lax.rem(p // 2 + step, X) + lax.rem(p, 2), yh, z)

    def y_line(step):
        other = lax.rem(u_me + step, NU)
        return at_chip(2 * (p // 2) + other // 2, lax.rem(other, 2), z)

    y_mate = at_chip(p, 1 - yh, z)

    def turn(depth):
        return lax.rem(depth, X) + (X // 2) * (depth // X)

    def held(row, depth, c):
        return c * Z + 2 * lax.rem(row // 2 + 2 * X - turn(depth), X) + lax.rem(row, 2)

    TWINS = 1
    mine = held(p, z, core)
    far = held(2 * lax.rem(p // 2 + X // 2, X) + lax.rem(p, 2), z, core)

    def a1_target(h2, twin):
        depth = h2 * X + p // 2
        row = 2 * lax.rem(z // 2 + turn(depth) + twin * (X // 2), X) + lax.rem(z, 2)
        return (row, (core * Z + depth) * 2 + yh)

    def a1_is_me(h2, twin):
        row, column = a1_target(h2, twin)
        return jnp.logical_and(row == p, column == q)

    def a1_source(half, twin):
        return (2 * lax.rem(z, X) + half, 2 * (far if twin else mine) + yh)

    def signal(where):
        pl.semaphore_signal(barrier, inc=1, device_id=where, device_id_type=MESH)

    barrier = pltpu.get_barrier_semaphore()
    signal(sibling)

    for step in range(1, X):
        signal(x_line(step))
    for step in range(1, NU):
        signal(y_line(step))

    @pl.loop(1, Z)
    def _(step):
        signal(at_chip(p, yh, lax.rem(z + step, Z)))

    expected = 1 + (X - 1) + (NU - 1) + (Z - 1)
    for twin in range(TWINS):
        for e in range(2):
            me = a1_is_me(e, twin)
            row, column = a1_source(e, twin)
            from_me = jnp.logical_and(row == p, column == q)

            @pl.when(jnp.logical_not(me))
            def _():
                signal(a1_target(e, twin))

            @pl.when(jnp.logical_not(from_me))
            def _():
                signal((row, column))

            expected = expected + jnp.where(me, 0, 1) + jnp.where(from_me, 0, 1)

    def copy(src, dst, send, recv, where):
        return pltpu.make_async_remote_copy(
            src_ref=src, dst_ref=dst, send_sem=send, recv_sem=recv,
            device_id=where, device_id_type=MESH,
        )

    def lanes(half, b):
        return pl.ds(pl.multiple_of((half * CT + b) * TILE, TILE), TILE)

    def m_local(b):
        return pltpu.make_async_copy(
            anc_ref.at[pl.ds(core * HALF, HALF), b], mfull.at[:, :, :, :, lanes(core, b)], m_l.at[b])

    def m_swap(b):
        return copy(
            anc_ref.at[pl.ds((1 - core) * HALF, HALF), b], mfull.at[:, :, :, :, lanes(core, b)],
            m_s.at[0], m_r.at[0], sibling)

    for b in range(CT):
        m_local(b).start()

    def keep(s, a):
        return mask_ref[s, a * NP + p].astype(F32)

    @pl.loop(0, SETS)
    def _(s):
        @pl.loop(0, RT)
        def _(a):
            mf[s, a] = panel_ref[s, a].astype(F32) * keep(s, a)

    rows = lax.broadcasted_iota(jnp.int32, (WH, W), 0)
    columns = lax.broadcasted_iota(jnp.int32, (WH, W), 1)
    hit = columns == (rows >> 1) * 4 + 2 * core + (rows & 1)
    perm[...] = jnp.where(hit, 1.0, 0.0).astype(BF16)

    pl.semaphore_wait(barrier, expected)

    def a0(s):
        return copy(mf.at[s], sib.at[s], a0_s.at[0], a0_r.at[s], sibling)

    for s in range(SETS):
        a0(s).start()
    for b in range(CT):
        m_swap(b).start()

    def l_slice(n, index):
        return lbuf.at[n, :, pl.ds(pl.multiple_of(16 * index, 16), 16), :]

    def l_bytes(n, count):
        return lbuf.at[n, :, pl.ds(0, 16 * count), :]

    def l_all(count):
        return lbuf.at[:, :, pl.ds(0, 16 * count), :]

    def a1_dst(s):
        return lbuf.at[
            pl.ds(s * PARTS, PARTS), pl.ds(lax.rem(p, 2) * CT, CT),
            pl.ds(pl.multiple_of(16 * chip, 16), 16), :]

    def a1(s, h2, twin):
        return copy(
            mpair.at[s, :, :, 2 * core + h2], a1_dst(s), a1_s.at[s, h2, twin], a1_r.at[s, twin],
            a1_target(h2, twin))

    def a1_local(s, h2, twin):
        return pltpu.make_async_copy(mpair.at[s, :, :, 2 * core + h2], a1_dst(s), a1_r.at[s, twin])

    def a1_wait(s, twin):
        index = far if twin else mine
        got = lbuf.at[pl.ds(s * PARTS, PARTS), :, pl.ds(pl.multiple_of(16 * index, 16), 16), :]
        copy(got, got, a1_s.at[s, 0, twin], a1_r.at[s, twin], sibling).wait_recv()

    @pl.loop(0, SETS)
    def _(s):
        a0(s).wait_recv()
        own = mf[s]
        other = sib[s]
        low = jnp.where(core == 0, own, other)
        high = jnp.where(core == 0, other, own)
        both = jnp.concatenate([low, high], axis=1).astype(BF16).reshape(CT, NH, 16, W)
        for w in range(PARTS):
            mpair[s, w] = both[..., w * WP : (w + 1) * WP]
        for twin in range(TWINS):
            for h2 in range(2):
                me = a1_is_me(h2, twin)

                @pl.when(me)
                def _():
                    a1_local(s, h2, twin).start()

                @pl.when(jnp.logical_not(me))
                def _():
                    a1(s, h2, twin).start()

    def transposed(s):
        total = jnp.zeros((WH, RT * 16), F32)
        for w in range(PARTS):
            total = total + lax.dot_general(
                perm[:, w * WP : (w + 1) * WP], mpair[s, w].reshape(RT * 16, WP),
                (((1,), (1,)), ((), ())), preferred_element_type=F32)
        mpt[s] = total.astype(BF16)

    def along(dx):
        return (2 * lax.rem(p // 2 + dx, X) + lax.rem(p, 2), q)

    over = (p + 1 - 2 * lax.rem(p, 2), q)

    def origin(step):
        row = lax.rem(p // 2 + X - step // 2, X)
        return held(2 * row + lax.rem(lax.rem(p, 2) + step, 2), z, core)

    def a2_over(n):
        return copy(l_slice(n, mine), l_slice(n, mine), l_s.at[0], a2_r.at[n, 1], over)

    def a2_over_far(n):
        return copy(l_slice(n, far), l_slice(n, far), l_s.at[0], a2_r.at[n, X + 1], over)

    NEAR = [dx for dx in range(1, X) if TWINS == 1 or dx != X // 2]
    LATER = [step for step in range(2, NP) if TWINS == 1 or step != X]

    def a2(n, dx, dy):
        index = mine if dy == 0 else held(over[0], z, core)
        return copy(l_slice(n, index), l_slice(n, index), l_s.at[0], a2_r.at[n, 2 * dx + dy], along(dx))

    def a2_wait(n, step):
        copy(l_slice(n, mine), l_slice(n, mine), l_s.at[0], a2_r.at[n, step], sibling).wait_recv()

    def a2_sibling(n):
        return copy(l_slice(n, mine), l_slice(n, mine), l_s.at[0], a3_r.at[n], sibling)

    def a3(n, step):
        index = origin(step)
        return copy(l_slice(n, index), l_slice(n, index), l_s.at[0], a3_r.at[n], sibling)

    def spread(n):
        @pl.when(lax.rem(n, PARTS) == 0)
        def _():
            a1_wait(n // PARTS, 0)

        a2_over(n).start()
        for dx in NEAR:
            a2(n, dx, 0).start()

        a2_sibling(n).start()
        if TWINS == 2:
            @pl.when(lax.rem(n, PARTS) == 0)
            def _():
                a1_wait(n // PARTS, 1)

            a2_over_far(n).start()
            a3(n, X).start()

    def relay(n):
        a2_wait(n, 1)
        for dx in NEAR:
            a2(n, dx, 1).start()

        a3(n, 1).start()

    @pl.loop(0, AHEAD)
    def _(n):
        spread(n)

    relay(0)

    def piece(n, depth, j):
        return (n, slice(None), slice(None), depth, slice(None), pl.ds(j * LC, LC))

    def y_piece(n, y, j):
        return (n, slice(None), y, z, slice(None), pl.ds(j * LC, LC))

    def pack(index, dst, count):
        groups = count // SUB
        top = jnp.zeros((SUB, LC), F32)
        for j in range(2):
            v = cbuf[index(j)].reshape(groups, SUB, LC)
            top = jnp.maximum(top, jnp.max(jnp.abs(v), axis=0))
        power = jnp.minimum(jnp.maximum(jnp.ceil(jnp.log2(top)), -100.0), 100.0)
        factor = jnp.exp2(-power) * LEVELS
        for j in range(2):
            v = cbuf[index(j)].reshape(groups, SUB, LC) * factor[None]
            whole = jnp.round(v).astype(jnp.int32).astype(I16)
            dst[pl.ds(j * count, count), :] = whole.reshape(count, LC)
        power = power.astype(jnp.int32)
        dst[pl.ds(2 * count, 16), :] = jnp.concatenate([power, power], axis=0).astype(I16)

    def scale_of(src, count):
        power = src[pl.ds(2 * count, 16), :].astype(jnp.int32).astype(F32)[:SUB]
        return jnp.exp2(power) * (1.0 / LEVELS)

    def unpack(src, scale, j, count):
        v = src[pl.ds(j * count, count), :].astype(jnp.int32).astype(F32)
        return v.reshape(count // SUB, SUB, LC) * scale[None]

    RING = HALF * 2 * 16
    MATE = HALF * 16

    def arm(n, way):
        return jnp.where(lax.rem(n, 2) == way, LONG, SHORT)

    def hop(n, way, k):
        step = 1 if way == 0 else Z - 1
        where = at_chip(p, yh, lax.rem(z + step, Z))
        slot = jnp.where(lax.rem(n, 2) == way, k, LONG + k)
        return copy(sbuf.at[n, slot], rbuf.at[n, slot], r_s.at[0], r_r.at[n, slot], where)

    def multiply(n, depth):
        product = jnp.dot(
            mfull[:, :, depth].reshape(RING, 2 * CT * TILE), lbuf[n].reshape(2 * CT * TILE, WP),
            preferred_element_type=F32)
        cbuf[n, :, :, depth] = product.reshape(HALF, 2, 16, WP)

    def ring_step(n, way, k):
        length = arm(n, way)
        left = length - k
        depth = lax.rem(z + Z + (left if way == 0 else -left), Z)

        @pl.when(k < length)
        def _():
            multiply(n, depth)

        @pl.when(jnp.logical_and(k > 0, k <= length))
        def _():
            hop(n, way, k - 1).wait_recv()
            src = rbuf.at[n, jnp.where(lax.rem(n, 2) == way, k - 1, LONG + k - 1)]
            scale = scale_of(src, RING)
            for j in range(2):
                index = piece(n, depth, j)
                shape = (HALF, 2, 16, LC)
                cbuf[index] = cbuf[index] + unpack(src, scale, j, RING).reshape(shape)

        @pl.when(k < length)
        def _():
            slot = jnp.where(lax.rem(n, 2) == way, k, LONG + k)
            pack(lambda j: piece(n, depth, j), sbuf.at[n, slot], RING)
            hop(n, way, k).start()

    def y_copy(n):
        return copy(ysb.at[n], yrb.at[n], y_s.at[0], y_r.at[n], y_mate)

    def c_copy(n):
        return copy(colp.at[n, core], colp.at[n, core], c_s.at[0], c_r.at[n], sibling)

    def arrive(n):
        @pl.when(n + 1 < COUNT)
        def _():
            relay(n + 1)

        @pl.when(n + AHEAD < COUNT)
        def _():
            spread(n + AHEAD)

        for step in LATER:
            a2_wait(n, step)
            a3(n, step).start()

        copy(l_bytes(n, NP), l_bytes(n, NP), l_s.at[0], a3_r.at[n], sibling).wait_recv()

        @pl.when(n == 0)
        def _():
            for s in range(SETS):
                transposed(s)

            for b in range(CT):
                m_local(b).wait()
            other = mfull.at[:, :, :, :, pl.ds(0, CT * TILE)]
            copy(other, other, m_s.at[0], m_r.at[0], sibling).wait_recv()

    def y_arrive(n):
        y_copy(n).wait_recv()
        src = yrb.at[n]
        scale = scale_of(src, MATE)
        for j in range(2):
            total = cbuf[y_piece(n, yh, j)] + unpack(src, scale, j, MATE).reshape(HALF, 16, LC)
            for a in range(HALF):
                image = -total[a] * keep(n // PARTS, core * HALF + a)
                colp[n, core, a, :, pl.ds(j * LC, LC)] = image.astype(BF16)
        c_copy(n).start()

    def d_copy(n, step):
        other = lax.rem(p // 2 + step, X)
        return copy(dsend.at[n, other], drecv.at[n, step], d_s.at[0], d_r.at[n], x_line(step))

    def f_copy(n, step):
        other = lax.rem(u_me + step, NU)
        return copy(fsend.at[n, other], frecv.at[n, step], f_s.at[0], f_r.at[n], y_line(step))

    def part_lanes(n):
        return pl.ds(pl.multiple_of(lax.rem(n, PARTS) * WP, WP), WP)

    def c_arrive(n):
        c_copy(n).wait_recv()
        dsend[n] = jnp.dot(
            mpt[n // PARTS], colp[n].reshape(RT * 16, WP), preferred_element_type=F32
        ).reshape(X, NU, 2 * Z, WP)
        for step in range(1, X):
            d_copy(n, step).start()

        both = colp[n].reshape(RT, 16, WP).astype(F32)
        picked = jnp.where(core == 0, both[:, :SUB], both[:, SUB:])
        col_ref[n // PARTS, :, :, part_lanes(n)] = picked.astype(BF16)

    def d_arrive(n):
        total = dsend[n, p // 2]
        if X > 1:
            got = drecv.at[n, pl.ds(1, X - 1)]
            copy(got, got, d_s.at[0], d_r.at[n], sibling).wait_recv()
            for step in range(1, X):
                total = total + drecv[n, step]
        fsend[n] = total
        for step in range(1, NU):
            f_copy(n, step).start()

    def f_arrive(n):
        got = frecv.at[n, pl.ds(1, NU - 1)]
        copy(got, got, f_s.at[0], f_r.at[n], sibling).wait_recv()
        total = fsend[n, u_me]
        for step in range(1, NU):
            total = total + frecv[n, step]
        for depth in range(Z):
            esend[depth, n // PARTS, :, part_lanes(n)] = total[2 * depth : 2 * depth + 2]

    @pl.loop(0, (COUNT - 1) * LAG + LONG + 5)
    def _(t):
        @pl.loop(0, COUNT)
        def _(n):
            k = t - n * LAG

            @pl.when(jnp.logical_and(k >= 1, k <= LONG))
            def _():
                for way in range(2):
                    ring_step(n, way, k)

            @pl.when(k == LONG)
            def _():
                pack(lambda j: y_piece(n, 1 - yh, j), ysb.at[n], MATE)
                y_copy(n).start()

        @pl.loop(0, COUNT)
        def _(n):
            k = t - n * LAG

            @pl.when(k == LONG + 4)
            def _():
                f_arrive(n)

            @pl.when(k == LONG + 3)
            def _():
                d_arrive(n)

            @pl.when(k == LONG + 2)
            def _():
                c_arrive(n)

            @pl.when(k == LONG + 1)
            def _():
                y_arrive(n)

            @pl.when(k == 0)
            def _():
                arrive(n)
                for way in range(2):
                    ring_step(n, way, k)
                multiply(n, z)

    def e_copy(step):
        other = lax.rem(z + step, Z)
        return copy(esend.at[other], erecv.at[step], e_s.at[0], e_r.at[0], at_chip(p, yh, other))

    @pl.loop(1, Z)
    def _(step):
        e_copy(step).start()

    got = erecv.at[pl.ds(1, Z - 1)]
    copy(got, got, e_s.at[0], e_r.at[0], sibling).wait_recv()
    total = esend[z]
    for step in range(1, Z):
        total = total + erecv[step]
    diag_ref[...] = dinv_ref[...] - total

    def sent(what, sem):
        copy(what, what, sem.at[0], sem.at[0], sibling).wait_send()

    sent(mfull.at[:, :, :, :, pl.ds(0, CT * TILE)], m_s)
    sent(mf, a0_s)
    sent(l_all(2 * NP - TWINS), l_s)
    sent(sbuf, r_s)
    sent(ysb, y_s)
    sent(colp.at[:, 0], c_s)
    if X > 1:
        sent(dsend.at[:, pl.ds(1, X - 1)], d_s)
    sent(fsend.at[:, pl.ds(1, NU - 1)], f_s)
    sent(got, e_s)

    @pl.loop(0, SETS)
    def _(s):
        for h2 in range(2):
            for twin in range(TWINS):
                @pl.when(jnp.logical_not(a1_is_me(h2, twin)))
                def _():
                    a1(s, h2, twin).wait_send()


def body(anc_inverse, panel, tile_mask, diag_inverse):
    n_row = lax.axis_size("prow")
    n_col = lax.axis_size("pcol")
    sets, rt, _, sub, w = panel.shape
    _, tile, ct, _ = anc_inverse.shape
    nz = n_col // 4
    anc = jnp.transpose(anc_inverse, (0, 2, 1, 3)).reshape(rt, ct, 2, nz, 16, tile)
    slim = panel.reshape(sets, rt, sub, w)
    half, nz, nh = rt // 2, n_col // 4, n_col // n_row
    wp, count = w // PARTS, sets * PARTS
    lc = wp // 2
    hops = nz - 1
    message = 2 * half * 2 * 16 + 16
    mate = 2 * half * 16 + 16
    dma = pltpu.SemaphoreType.DMA
    vmem = pl.BlockSpec(memory_space=pltpu.VMEM)
    scratch = [
        pltpu.VMEM((half, 2, nz, 16, 2 * ct * tile), BF16),
        pltpu.VMEM((sets, rt, sub, w), F32),
        pltpu.VMEM((sets, rt, sub, w), F32),
        pltpu.VMEM((sets, PARTS, ct, nh, 16, wp), BF16),
        pltpu.VMEM((count, 2 * ct, tile, wp), BF16),
        pltpu.VMEM((count, half, 2, nz, 16, wp), F32),
        pltpu.VMEM((count, hops, message, lc), I16),
        pltpu.VMEM((count, hops, message, lc), I16),
        pltpu.VMEM((count, mate, lc), I16),
        pltpu.VMEM((count, mate, lc), I16),
        pltpu.VMEM((count, 2, half, 16, wp), BF16),
        pltpu.VMEM((w // 2, w), BF16),
        pltpu.VMEM((sets, w // 2, rt * 16), BF16),
        pltpu.VMEM((count, n_row // 2, 4, 2 * nz, wp), F32),
        pltpu.VMEM((count, n_row // 2, 4, 2 * nz, wp), F32),
        pltpu.VMEM((count, 4, 2 * nz, wp), F32),
        pltpu.VMEM((count, 4, 2 * nz, wp), F32),
        pltpu.VMEM((nz, sets, 2, w), F32),
        pltpu.VMEM((nz, sets, 2, w), F32),
        dma((ct,)), dma((1,)), dma((1,)),
        dma((1,)), dma((sets,)),
        dma((sets, 2, 2)), dma((sets, 2)),
        dma((1,)), dma((count, n_row)), dma((count,)),
        dma((1,)), dma((count, hops)),
        dma((1,)), dma((count,)),
        dma((1,)), dma((count,)),
        dma((1,)), dma((count,)),
        dma((1,)), dma((count,)),
        dma((1,)), dma((1,)),
    ]
    column, diag = pl.pallas_call(
        functools.partial(kernel, n_row, n_col),
        out_shape=(
            jax.ShapeDtypeStruct((sets, rt, sub, w), BF16),
            jax.ShapeDtypeStruct(diag_inverse.shape, F32),
        ),
        in_specs=[
            pl.BlockSpec(memory_space=pltpu.SMEM),
            pl.BlockSpec(memory_space=pl.ANY),
            vmem,
            vmem,
        ],
        out_specs=(vmem, vmem),
        scratch_shapes=scratch,
        compiler_params=pltpu.CompilerParams(
            collective_id=0, has_side_effects=True, vmem_limit_bytes=56 * 1024 * 1024
        ),
        name="selected_inverse",
    )(tile_mask, anc, slim, diag_inverse)
    return column.reshape(panel.shape), diag


def solution(mesh):
    in_specs = (
        P(None, "prow", None, "pcol"),
        P(None, None, "prow", "pcol", None),
        P(),
        P(None, ("prow", "pcol"), None),
    )
    out_specs = (P(None, None, "prow", "pcol", None), P(None, ("prow", "pcol"), None))
    return jax.shard_map(body, mesh=mesh, in_specs=in_specs, out_specs=out_specs, check_vma=False)
```

```python
import functools

import jax
import jax.numpy as jnp
from jax import lax
from jax.experimental import pallas as pl
from jax.experimental.pallas import tpu as pltpu
from jax.sharding import PartitionSpec as P

MESH = pl.DeviceIdType.MESH
F32 = jnp.float32
BF16 = jnp.bfloat16
I16 = jnp.int16
SUB = 8
LEVELS = 32000.0
PARTS = 2
LAG = 1
AHEAD = 2


def kernel(
    NP, NCOL, mask_ref, anc_ref, panel_ref, dinv_ref, col_ref, diag_ref,
    mfull, mf, sib, mpair, lbuf, cbuf, sbuf, rbuf, ysb, yrb, colp, perm, mpt,
    dsend, drecv, fsend, frecv, esend, erecv,
    m_l, m_s, m_r, a0_s, a0_r, a1_s, a1_r, l_s, a2_r, a3_r,
    r_s, r_r, y_s, y_r, c_s, c_r, d_s, d_r, f_s, f_r, e_s, e_r,
):
    SETS, RT, _, W = panel_ref.shape
    CT = anc_ref.shape[1]
    TILE = anc_ref.shape[-1]
    HALF = RT // 2
    NC = NCOL // 2
    Z = NC // 2
    NH = NCOL // NP
    WP = W // PARTS
    COUNT = SETS * PARTS
    LC = WP // 2
    WH = W // 2
    X = NP // 2
    NU = 4
    LONG = Z // 2
    SHORT = Z - 1 - LONG

    p = lax.axis_index("prow")
    q = lax.axis_index("pcol")
    core = lax.rem(q, 2)
    chip = q // 2
    z = lax.rem(chip, Z)
    yh = chip // Z
    sibling = (p, q + 1 - 2 * core)

    def at_chip(row, y, depth):
        return (row, (y * Z + depth) * 2 + core)

    u_me = lax.rem(p, 2) * 2 + yh

    def x_line(step):
        return at_chip(2 * lax.rem(p // 2 + step, X) + lax.rem(p, 2), yh, z)

    def y_line(step):
        other = lax.rem(u_me + step, NU)
        return at_chip(2 * (p // 2) + other // 2, lax.rem(other, 2), z)

    y_mate = at_chip(p, 1 - yh, z)

    def turn(depth):
        return lax.rem(depth, X) + (X // 2) * (depth // X)

    def held(row, depth, c):
        return c * Z + 2 * lax.rem(row // 2 + 2 * X - turn(depth), X) + lax.rem(row, 2)

    TWINS = 1
    mine = held(p, z, core)
    far = held(2 * lax.rem(p // 2 + X // 2, X) + lax.rem(p, 2), z, core)

    def a1_target(h2, twin):
        depth = h2 * X + p // 2
        row = 2 * lax.rem(z // 2 + turn(depth) + twin * (X // 2), X) + lax.rem(z, 2)
        return (row, (core * Z + depth) * 2 + yh)

    def a1_is_me(h2, twin):
        row, column = a1_target(h2, twin)
        return jnp.logical_and(row == p, column == q)

    def a1_source(half, twin):
        return (2 * lax.rem(z, X) + half, 2 * (far if twin else mine) + yh)

    def signal(where):
        pl.semaphore_signal(barrier, inc=1, device_id=where, device_id_type=MESH)

    barrier = pltpu.get_barrier_semaphore()
    signal(sibling)

    for step in range(1, X):
        signal(x_line(step))
    for step in range(1, NU):
        signal(y_line(step))
    for step in range(3, NP, 2):
        signal((2 * lax.rem(p // 2 + step // 2, X) + lax.rem(p + 1, 2), q))


    @pl.loop(1, Z)
    def _(step):
        signal(at_chip(p, yh, lax.rem(z + step, Z)))

    expected = 1 + 2 * (X - 1) + (NU - 1) + (Z - 1)
    for twin in range(TWINS):
        for e in range(2):
            me = a1_is_me(e, twin)
            row, column = a1_source(e, twin)
            from_me = jnp.logical_and(row == p, column == q)

            @pl.when(jnp.logical_not(me))
            def _():
                signal(a1_target(e, twin))

            @pl.when(jnp.logical_not(from_me))
            def _():
                signal((row, column))

            expected = expected + jnp.where(me, 0, 1) + jnp.where(from_me, 0, 1)

    def copy(src, dst, send, recv, where):
        return pltpu.make_async_remote_copy(
            src_ref=src, dst_ref=dst, send_sem=send, recv_sem=recv,
            device_id=where, device_id_type=MESH,
        )

    def lanes(half, b):
        return pl.ds(pl.multiple_of((half * CT + b) * TILE, TILE), TILE)

    def m_local(b):
        return pltpu.make_async_copy(
            anc_ref.at[pl.ds(core * HALF, HALF), b], mfull.at[:, :, :, :, lanes(core, b)], m_l.at[b])

    def m_swap(b):
        return copy(
            anc_ref.at[pl.ds((1 - core) * HALF, HALF), b], mfull.at[:, :, :, :, lanes(core, b)],
            m_s.at[0], m_r.at[0], sibling)

    for b in range(CT):
        m_local(b).start()

    def keep(s, a):
        return mask_ref[s, a * NP + p].astype(F32)

    @pl.loop(0, SETS)
    def _(s):
        @pl.loop(0, RT)
        def _(a):
            mf[s, a] = panel_ref[s, a].astype(F32) * keep(s, a)

    rows = lax.broadcasted_iota(jnp.int32, (WH, W), 0)
    columns = lax.broadcasted_iota(jnp.int32, (WH, W), 1)
    hit = columns == (rows >> 1) * 4 + 2 * core + (rows & 1)
    perm[...] = jnp.where(hit, 1.0, 0.0).astype(BF16)

    pl.semaphore_wait(barrier, expected)

    def a0(s):
        return copy(mf.at[s], sib.at[s], a0_s.at[0], a0_r.at[s], sibling)

    for s in range(SETS):
        a0(s).start()
    for b in range(CT):
        m_swap(b).start()

    def l_slice(n, index):
        return lbuf.at[n, :, pl.ds(pl.multiple_of(16 * index, 16), 16), :]

    def l_bytes(n, count):
        return lbuf.at[n, :, pl.ds(0, 16 * count), :]

    def l_all(count):
        return lbuf.at[:, :, pl.ds(0, 16 * count), :]

    def a1_dst(s):
        return lbuf.at[
            pl.ds(s * PARTS, PARTS), pl.ds(lax.rem(p, 2) * CT, CT),
            pl.ds(pl.multiple_of(16 * chip, 16), 16), :]

    def a1(s, h2, twin):
        return copy(
            mpair.at[s, :, :, 2 * core + h2], a1_dst(s), a1_s.at[s, h2, twin], a1_r.at[s, twin],
            a1_target(h2, twin))

    def a1_local(s, h2, twin):
        return pltpu.make_async_copy(mpair.at[s, :, :, 2 * core + h2], a1_dst(s), a1_r.at[s, twin])

    def a1_wait(s, twin):
        index = far if twin else mine
        got = lbuf.at[pl.ds(s * PARTS, PARTS), :, pl.ds(pl.multiple_of(16 * index, 16), 16), :]
        copy(got, got, a1_s.at[s, 0, twin], a1_r.at[s, twin], sibling).wait_recv()

    @pl.loop(0, SETS)
    def _(s):
        a0(s).wait_recv()
        own = mf[s]
        other = sib[s]
        low = jnp.where(core == 0, own, other)
        high = jnp.where(core == 0, other, own)
        both = jnp.concatenate([low, high], axis=1).astype(BF16).reshape(CT, NH, 16, W)
        for w in range(PARTS):
            mpair[s, w] = both[..., w * WP : (w + 1) * WP]
        for twin in range(TWINS):
            for h2 in range(2):
                me = a1_is_me(h2, twin)

                @pl.when(me)
                def _():
                    a1_local(s, h2, twin).start()

                @pl.when(jnp.logical_not(me))
                def _():
                    a1(s, h2, twin).start()

    def transposed(s):
        total = jnp.zeros((WH, RT * 16), F32)
        for w in range(PARTS):
            total = total + lax.dot_general(
                perm[:, w * WP : (w + 1) * WP], mpair[s, w].reshape(RT * 16, WP),
                (((1,), (1,)), ((), ())), preferred_element_type=F32)
        mpt[s] = total.astype(BF16)

    def across(step):
        return (2 * lax.rem(p // 2 + step // 2, X) + lax.rem(p + step, 2), q)

    def origin(step):
        row = lax.rem(p // 2 + X - step // 2, X)
        return held(2 * row + lax.rem(p + step, 2), z, core)

    def a2(n, step):
        return copy(l_slice(n, mine), l_slice(n, mine), l_s.at[0], a2_r.at[n, step], across(step))

    def a2_wait(n, step):
        copy(l_slice(n, mine), l_slice(n, mine), l_s.at[0], a2_r.at[n, step], sibling).wait_recv()

    def a2_sibling(n):
        return copy(l_slice(n, mine), l_slice(n, mine), l_s.at[0], a3_r.at[n], sibling)

    def a3(n, step):
        index = origin(step)
        return copy(l_slice(n, index), l_slice(n, index), l_s.at[0], a3_r.at[n], sibling)

    def spread(n):
        @pl.when(lax.rem(n, PARTS) == 0)
        def _():
            a1_wait(n // PARTS, 0)

        for step in range(1, NP):
            a2(n, step).start()

        a2_sibling(n).start()

    @pl.loop(0, AHEAD)
    def _(n):
        spread(n)

    def piece(n, depth, j):
        return (n, slice(None), slice(None), depth, slice(None), pl.ds(j * LC, LC))

    def y_piece(n, y, j):
        return (n, slice(None), y, z, slice(None), pl.ds(j * LC, LC))

    def pack(index, dst, count):
        groups = count // SUB
        top = jnp.zeros((SUB, LC), F32)
        for j in range(2):
            v = cbuf[index(j)].reshape(groups, SUB, LC)
            top = jnp.maximum(top, jnp.max(jnp.abs(v), axis=0))
        power = jnp.minimum(jnp.maximum(jnp.ceil(jnp.log2(top)), -100.0), 100.0)
        factor = jnp.exp2(-power) * LEVELS
        for j in range(2):
            v = cbuf[index(j)].reshape(groups, SUB, LC) * factor[None]
            whole = jnp.round(v).astype(jnp.int32).astype(I16)
            dst[pl.ds(j * count, count), :] = whole.reshape(count, LC)
        power = power.astype(jnp.int32)
        dst[pl.ds(2 * count, 16), :] = jnp.concatenate([power, power], axis=0).astype(I16)

    def scale_of(src, count):
        power = src[pl.ds(2 * count, 16), :].astype(jnp.int32).astype(F32)[:SUB]
        return jnp.exp2(power) * (1.0 / LEVELS)

    def unpack(src, scale, j, count):
        v = src[pl.ds(j * count, count), :].astype(jnp.int32).astype(F32)
        return v.reshape(count // SUB, SUB, LC) * scale[None]

    RING = HALF * 2 * 16
    MATE = HALF * 16

    def arm(n, way):
        return jnp.where(lax.rem(n, 2) == way, LONG, SHORT)

    def hop(n, way, k):
        step = 1 if way == 0 else Z - 1
        where = at_chip(p, yh, lax.rem(z + step, Z))
        slot = jnp.where(lax.rem(n, 2) == way, k, LONG + k)
        return copy(sbuf.at[n, slot], rbuf.at[n, slot], r_s.at[0], r_r.at[n, slot], where)

    def multiply(n, depth):
        product = jnp.dot(
            mfull[:, :, depth].reshape(RING, 2 * CT * TILE), lbuf[n].reshape(2 * CT * TILE, WP),
            preferred_element_type=F32)
        cbuf[n, :, :, depth] = product.reshape(HALF, 2, 16, WP)

    def ring_step(n, way, k):
        length = arm(n, way)
        left = length - k
        depth = lax.rem(z + Z + (left if way == 0 else -left), Z)

        @pl.when(k < length)
        def _():
            multiply(n, depth)

        @pl.when(jnp.logical_and(k > 0, k <= length))
        def _():
            hop(n, way, k - 1).wait_recv()
            src = rbuf.at[n, jnp.where(lax.rem(n, 2) == way, k - 1, LONG + k - 1)]
            scale = scale_of(src, RING)
            for j in range(2):
                index = piece(n, depth, j)
                shape = (HALF, 2, 16, LC)
                cbuf[index] = cbuf[index] + unpack(src, scale, j, RING).reshape(shape)

        @pl.when(k < length)
        def _():
            slot = jnp.where(lax.rem(n, 2) == way, k, LONG + k)
            pack(lambda j: piece(n, depth, j), sbuf.at[n, slot], RING)
            hop(n, way, k).start()

    def y_copy(n):
        return copy(ysb.at[n], yrb.at[n], y_s.at[0], y_r.at[n], y_mate)

    def c_copy(n):
        return copy(colp.at[n, core], colp.at[n, core], c_s.at[0], c_r.at[n], sibling)

    def arrive(n):
        for step in range(1, NP):
            a2_wait(n, step)
            a3(n, step).start()

        @pl.when(n + AHEAD < COUNT)
        def _():
            spread(n + AHEAD)

        copy(l_bytes(n, NP), l_bytes(n, NP), l_s.at[0], a3_r.at[n], sibling).wait_recv()

        @pl.when(n == 0)
        def _():
            for b in range(CT):
                m_local(b).wait()
            other = mfull.at[:, :, :, :, pl.ds(0, CT * TILE)]
            copy(other, other, m_s.at[0], m_r.at[0], sibling).wait_recv()

    def y_arrive(n):
        y_copy(n).wait_recv()
        src = yrb.at[n]
        scale = scale_of(src, MATE)
        for j in range(2):
            total = cbuf[y_piece(n, yh, j)] + unpack(src, scale, j, MATE).reshape(HALF, 16, LC)
            for a in range(HALF):
                image = -total[a] * keep(n // PARTS, core * HALF + a)
                colp[n, core, a, :, pl.ds(j * LC, LC)] = image.astype(BF16)
        c_copy(n).start()

    def d_copy(n, step):
        other = lax.rem(p // 2 + step, X)
        return copy(dsend.at[n, other], drecv.at[n, step], d_s.at[0], d_r.at[n], x_line(step))

    def f_copy(n, step):
        other = lax.rem(u_me + step, NU)
        return copy(fsend.at[n, other], frecv.at[n, step], f_s.at[0], f_r.at[n], y_line(step))

    def part_lanes(n):
        return pl.ds(pl.multiple_of(lax.rem(n, PARTS) * WP, WP), WP)

    def c_arrive(n):
        c_copy(n).wait_recv()
        dsend[n] = jnp.dot(
            mpt[n // PARTS], colp[n].reshape(RT * 16, WP), preferred_element_type=F32
        ).reshape(X, NU, 2 * Z, WP)
        for step in range(1, X):
            d_copy(n, step).start()

        both = colp[n].reshape(RT, 16, WP).astype(F32)
        picked = jnp.where(core == 0, both[:, :SUB], both[:, SUB:])
        col_ref[n // PARTS, :, :, part_lanes(n)] = picked.astype(BF16)

    def d_arrive(n):
        total = dsend[n, p // 2]
        if X > 1:
            got = drecv.at[n, pl.ds(1, X - 1)]
            copy(got, got, d_s.at[0], d_r.at[n], sibling).wait_recv()
            for step in range(1, X):
                total = total + drecv[n, step]
        fsend[n] = total
        for step in range(1, NU):
            f_copy(n, step).start()

    def f_arrive(n):
        got = frecv.at[n, pl.ds(1, NU - 1)]
        copy(got, got, f_s.at[0], f_r.at[n], sibling).wait_recv()
        total = fsend[n, u_me]
        for step in range(1, NU):
            total = total + frecv[n, step]
        for depth in range(Z):
            esend[depth, n // PARTS, :, part_lanes(n)] = total[2 * depth : 2 * depth + 2]

    @pl.loop(0, (COUNT - 1) * LAG + LONG + 5)
    def _(t):
        @pl.loop(0, COUNT)
        def _(n):
            k = t - n * LAG

            @pl.when(jnp.logical_and(k >= 1, k <= LONG))
            def _():
                for way in range(2):
                    ring_step(n, way, k)

            @pl.when(k == LONG)
            def _():
                pack(lambda j: y_piece(n, 1 - yh, j), ysb.at[n], MATE)
                y_copy(n).start()

        @pl.loop(0, COUNT)
        def _(n):
            k = t - n * LAG

            @pl.when(k == LONG + 4)
            def _():
                f_arrive(n)

            @pl.when(k == LONG + 3)
            def _():
                d_arrive(n)

            @pl.when(k == LONG + 2)
            def _():
                c_arrive(n)

            @pl.when(k == LONG + 1)
            def _():
                y_arrive(n)

            @pl.when(k == 0)
            def _():
                arrive(n)
                for way in range(2):
                    ring_step(n, way, k)
                multiply(n, z)

                @pl.when(n == 0)
                def _():
                    for s in range(SETS):
                        transposed(s)

    def e_copy(step):
        other = lax.rem(z + step, Z)
        return copy(esend.at[other], erecv.at[step], e_s.at[0], e_r.at[0], at_chip(p, yh, other))

    @pl.loop(1, Z)
    def _(step):
        e_copy(step).start()

    got = erecv.at[pl.ds(1, Z - 1)]
    copy(got, got, e_s.at[0], e_r.at[0], sibling).wait_recv()
    total = esend[z]
    for step in range(1, Z):
        total = total + erecv[step]
    diag_ref[...] = dinv_ref[...] - total

    def sent(what, sem):
        copy(what, what, sem.at[0], sem.at[0], sibling).wait_send()

    sent(mfull.at[:, :, :, :, pl.ds(0, CT * TILE)], m_s)
    sent(mf, a0_s)
    sent(l_all(2 * NP - TWINS), l_s)
    sent(sbuf, r_s)
    sent(ysb, y_s)
    sent(colp.at[:, 0], c_s)
    if X > 1:
        sent(dsend.at[:, pl.ds(1, X - 1)], d_s)
    sent(fsend.at[:, pl.ds(1, NU - 1)], f_s)
    sent(got, e_s)

    @pl.loop(0, SETS)
    def _(s):
        for h2 in range(2):
            for twin in range(TWINS):
                @pl.when(jnp.logical_not(a1_is_me(h2, twin)))
                def _():
                    a1(s, h2, twin).wait_send()


def body(anc_inverse, panel, tile_mask, diag_inverse):
    n_row = lax.axis_size("prow")
    n_col = lax.axis_size("pcol")
    sets, rt, _, sub, w = panel.shape
    _, tile, ct, _ = anc_inverse.shape
    nz = n_col // 4
    anc = jnp.transpose(anc_inverse, (0, 2, 1, 3)).reshape(rt, ct, 2, nz, 16, tile)
    slim = panel.reshape(sets, rt, sub, w)
    half, nz, nh = rt // 2, n_col // 4, n_col // n_row
    wp, count = w // PARTS, sets * PARTS
    lc = wp // 2
    hops = nz - 1
    message = 2 * half * 2 * 16 + 16
    mate = 2 * half * 16 + 16
    dma = pltpu.SemaphoreType.DMA
    vmem = pl.BlockSpec(memory_space=pltpu.VMEM)
    scratch = [
        pltpu.VMEM((half, 2, nz, 16, 2 * ct * tile), BF16),
        pltpu.VMEM((sets, rt, sub, w), F32),
        pltpu.VMEM((sets, rt, sub, w), F32),
        pltpu.VMEM((sets, PARTS, ct, nh, 16, wp), BF16),
        pltpu.VMEM((count, 2 * ct, tile, wp), BF16),
        pltpu.VMEM((count, half, 2, nz, 16, wp), F32),
        pltpu.VMEM((count, hops, message, lc), I16),
        pltpu.VMEM((count, hops, message, lc), I16),
        pltpu.VMEM((count, mate, lc), I16),
        pltpu.VMEM((count, mate, lc), I16),
        pltpu.VMEM((count, 2, half, 16, wp), BF16),
        pltpu.VMEM((w // 2, w), BF16),
        pltpu.VMEM((sets, w // 2, rt * 16), BF16),
        pltpu.VMEM((count, n_row // 2, 4, 2 * nz, wp), F32),
        pltpu.VMEM((count, n_row // 2, 4, 2 * nz, wp), F32),
        pltpu.VMEM((count, 4, 2 * nz, wp), F32),
        pltpu.VMEM((count, 4, 2 * nz, wp), F32),
        pltpu.VMEM((nz, sets, 2, w), F32),
        pltpu.VMEM((nz, sets, 2, w), F32),
        dma((ct,)), dma((1,)), dma((1,)),
        dma((1,)), dma((sets,)),
        dma((sets, 2, 2)), dma((sets, 2)),
        dma((1,)), dma((count, n_row)), dma((count,)),
        dma((1,)), dma((count, hops)),
        dma((1,)), dma((count,)),
        dma((1,)), dma((count,)),
        dma((1,)), dma((count,)),
        dma((1,)), dma((count,)),
        dma((1,)), dma((1,)),
    ]
    column, diag = pl.pallas_call(
        functools.partial(kernel, n_row, n_col),
        out_shape=(
            jax.ShapeDtypeStruct((sets, rt, sub, w), BF16),
            jax.ShapeDtypeStruct(diag_inverse.shape, F32),
        ),
        in_specs=[
            pl.BlockSpec(memory_space=pltpu.SMEM),
            pl.BlockSpec(memory_space=pl.ANY),
            vmem,
            vmem,
        ],
        out_specs=(vmem, vmem),
        scratch_shapes=scratch,
        compiler_params=pltpu.CompilerParams(
            collective_id=0, has_side_effects=True, vmem_limit_bytes=56 * 1024 * 1024
        ),
        name="selected_inverse",
    )(tile_mask, anc, slim, diag_inverse)
    return column.reshape(panel.shape), diag


def solution(mesh):
    in_specs = (
        P(None, "prow", None, "pcol"),
        P(None, None, "prow", "pcol", None),
        P(),
        P(None, ("prow", "pcol"), None),
    )
    out_specs = (P(None, None, "prow", "pcol", None), P(None, ("prow", "pcol"), None))
    return jax.shard_map(body, mesh=mesh, in_specs=in_specs, out_specs=out_specs, check_vma=False)
```

```python
import functools

import jax
import jax.numpy as jnp
from jax import lax
from jax.experimental import pallas as pl
from jax.experimental.pallas import tpu as pltpu
from jax.sharding import PartitionSpec as P

MESH = pl.DeviceIdType.MESH
F32 = jnp.float32
BF16 = jnp.bfloat16
I16 = jnp.int16
SUB = 8
LEVELS = 32000.0
PARTS = 2
LAG = 1
AHEAD = 2


def kernel(
    NP, NCOL, mask_ref, anc_ref, panel_ref, dinv_ref, col_ref, diag_ref,
    mfull, mf, sib, mpair, lbuf, cbuf, sbuf, rbuf, ysb, yrb, colp, perm, mpt,
    dsend, drecv, fsend, frecv, esend, erecv,
    m_l, m_s, m_r, a0_s, a0_r, a1_s, a1_r, l_s, a2_r, a3_r,
    r_s, r_r, y_s, y_r, c_s, c_r, d_s, d_r, f_s, f_r, e_s, e_r,
):
    SETS, RT, _, W = panel_ref.shape
    CT = anc_ref.shape[1]
    TILE = anc_ref.shape[-1]
    HALF = RT // 2
    NC = NCOL // 2
    Z = NC // 2
    NH = NCOL // NP
    WP = W // PARTS
    COUNT = SETS * PARTS
    LC = WP // 2
    WH = W // 2
    X = NP // 2
    NU = 4
    LONG = Z // 2
    SHORT = Z - 1 - LONG

    p = lax.axis_index("prow")
    q = lax.axis_index("pcol")
    core = lax.rem(q, 2)
    chip = q // 2
    z = lax.rem(chip, Z)
    yh = chip // Z
    sibling = (p, q + 1 - 2 * core)

    def at_chip(row, y, depth):
        return (row, (y * Z + depth) * 2 + core)

    u_me = lax.rem(p, 2) * 2 + yh

    def x_line(step):
        return at_chip(2 * lax.rem(p // 2 + step, X) + lax.rem(p, 2), yh, z)

    def y_line(step):
        other = lax.rem(u_me + step, NU)
        return at_chip(2 * (p // 2) + other // 2, lax.rem(other, 2), z)

    y_mate = at_chip(p, 1 - yh, z)

    def turn(depth):
        return lax.rem(depth, X) + (X // 2) * (depth // X)

    def held(row, depth, c):
        return c * Z + 2 * lax.rem(row // 2 + 2 * X - turn(depth), X) + lax.rem(row, 2)

    TWINS = 1
    mine = held(p, z, core)
    far = held(2 * lax.rem(p // 2 + X // 2, X) + lax.rem(p, 2), z, core)

    def a1_target(h2, twin):
        depth = h2 * X + p // 2
        row = 2 * lax.rem(z // 2 + turn(depth) + twin * (X // 2), X) + lax.rem(z, 2)
        return (row, (core * Z + depth) * 2 + yh)

    def a1_is_me(h2, twin):
        row, column = a1_target(h2, twin)
        return jnp.logical_and(row == p, column == q)

    def a1_source(half, twin):
        return (2 * lax.rem(z, X) + half, 2 * (far if twin else mine) + yh)

    def signal(where):
        pl.semaphore_signal(barrier, inc=1, device_id=where, device_id_type=MESH)

    barrier = pltpu.get_barrier_semaphore()
    signal(sibling)

    for step in range(1, X):
        signal(x_line(step))
    for step in range(1, NU):
        signal(y_line(step))
    for step in range(3, NP, 2):
        signal((2 * lax.rem(p // 2 + step // 2, X) + lax.rem(p + 1, 2), q))


    @pl.loop(1, Z)
    def _(step):
        signal(at_chip(p, yh, lax.rem(z + step, Z)))

    expected = 1 + 2 * (X - 1) + (NU - 1) + (Z - 1)
    for twin in range(TWINS):
        for e in range(2):
            me = a1_is_me(e, twin)
            row, column = a1_source(e, twin)
            from_me = jnp.logical_and(row == p, column == q)

            @pl.when(jnp.logical_not(me))
            def _():
                signal(a1_target(e, twin))

            @pl.when(jnp.logical_not(from_me))
            def _():
                signal((row, column))

            expected = expected + jnp.where(me, 0, 1) + jnp.where(from_me, 0, 1)

    def copy(src, dst, send, recv, where):
        return pltpu.make_async_remote_copy(
            src_ref=src, dst_ref=dst, send_sem=send, recv_sem=recv,
            device_id=where, device_id_type=MESH,
        )

    def lanes(half, b):
        return pl.ds(pl.multiple_of((half * CT + b) * TILE, TILE), TILE)

    def m_local(b):
        return pltpu.make_async_copy(
            anc_ref.at[pl.ds(core * HALF, HALF), b], mfull.at[:, :, :, :, lanes(core, b)], m_l.at[b])

    def m_swap(b):
        return copy(
            anc_ref.at[pl.ds((1 - core) * HALF, HALF), b], mfull.at[:, :, :, :, lanes(core, b)],
            m_s.at[0], m_r.at[0], sibling)

    for b in range(CT):
        m_local(b).start()

    def keep(s, a):
        return mask_ref[s, a * NP + p].astype(F32)

    @pl.loop(0, SETS)
    def _(s):
        @pl.loop(0, RT)
        def _(a):
            mf[s, a] = panel_ref[s, a].astype(F32) * keep(s, a)

    rows = lax.broadcasted_iota(jnp.int32, (WH, W), 0)
    columns = lax.broadcasted_iota(jnp.int32, (WH, W), 1)
    hit = columns == (rows >> 1) * 4 + 2 * core + (rows & 1)
    perm[...] = jnp.where(hit, 1.0, 0.0).astype(BF16)

    pl.semaphore_wait(barrier, expected)

    def a0(s):
        return copy(mf.at[s], sib.at[s], a0_s.at[0], a0_r.at[s], sibling)

    for s in range(SETS):
        a0(s).start()
    for b in range(CT):
        m_swap(b).start()

    def l_slice(n, index):
        return lbuf.at[n, :, pl.ds(pl.multiple_of(16 * index, 16), 16), :]

    def l_bytes(n, count):
        return lbuf.at[n, :, pl.ds(0, 16 * count), :]

    def l_all(count):
        return lbuf.at[:, :, pl.ds(0, 16 * count), :]

    def a1_dst(s):
        return lbuf.at[
            pl.ds(s * PARTS, PARTS), pl.ds(lax.rem(p, 2) * CT, CT),
            pl.ds(pl.multiple_of(16 * chip, 16), 16), :]

    def a1(s, h2, twin):
        return copy(
            mpair.at[s, :, :, 2 * core + h2], a1_dst(s), a1_s.at[s, h2, twin], a1_r.at[s, twin],
            a1_target(h2, twin))

    def a1_local(s, h2, twin):
        return pltpu.make_async_copy(mpair.at[s, :, :, 2 * core + h2], a1_dst(s), a1_r.at[s, twin])

    def a1_wait(s, twin):
        index = far if twin else mine
        got = lbuf.at[pl.ds(s * PARTS, PARTS), :, pl.ds(pl.multiple_of(16 * index, 16), 16), :]
        copy(got, got, a1_s.at[s, 0, twin], a1_r.at[s, twin], sibling).wait_recv()

    @pl.loop(0, SETS)
    def _(s):
        a0(s).wait_recv()
        own = mf[s]
        other = sib[s]
        low = jnp.where(core == 0, own, other)
        high = jnp.where(core == 0, other, own)
        both = jnp.concatenate([low, high], axis=1).astype(BF16).reshape(CT, NH, 16, W)
        for w in range(PARTS):
            mpair[s, w] = both[..., w * WP : (w + 1) * WP]
        for twin in range(TWINS):
            for h2 in range(2):
                me = a1_is_me(h2, twin)

                @pl.when(me)
                def _():
                    a1_local(s, h2, twin).start()

                @pl.when(jnp.logical_not(me))
                def _():
                    a1(s, h2, twin).start()

    def transposed(s):
        total = jnp.zeros((WH, RT * 16), F32)
        for w in range(PARTS):
            total = total + lax.dot_general(
                perm[:, w * WP : (w + 1) * WP], mpair[s, w].reshape(RT * 16, WP),
                (((1,), (1,)), ((), ())), preferred_element_type=F32)
        mpt[s] = total.astype(BF16)

    def across(step):
        return (2 * lax.rem(p // 2 + step // 2, X) + lax.rem(p + step, 2), q)

    def origin(step):
        row = lax.rem(p // 2 + X - step // 2, X)
        return held(2 * row + lax.rem(p + step, 2), z, core)

    def a2(n, step):
        return copy(l_slice(n, mine), l_slice(n, mine), l_s.at[0], a2_r.at[n, step], across(step))

    def a2_wait(n, step):
        copy(l_slice(n, mine), l_slice(n, mine), l_s.at[0], a2_r.at[n, step], sibling).wait_recv()

    def a2_sibling(n):
        return copy(l_slice(n, mine), l_slice(n, mine), l_s.at[0], a3_r.at[n], sibling)

    def a3(n, step):
        index = origin(step)
        return copy(l_slice(n, index), l_slice(n, index), l_s.at[0], a3_r.at[n], sibling)

    FAR = [step for step in range(1, NP) if X > 1 and step // 2 == X // 2]
    CLOSE = [step for step in range(1, NP) if step not in FAR]

    def spread(n):
        @pl.when(lax.rem(n, PARTS) == 0)
        def _():
            a1_wait(n // PARTS, 0)

        for step in FAR + CLOSE[1:] + CLOSE[:1]:
            a2(n, step).start()

        a2_sibling(n).start()

    @pl.loop(0, AHEAD)
    def _(n):
        spread(n)

    def piece(n, depth, j):
        return (n, slice(None), slice(None), depth, slice(None), pl.ds(j * LC, LC))

    def y_piece(n, y, j):
        return (n, slice(None), y, z, slice(None), pl.ds(j * LC, LC))

    def pack(index, dst, count):
        groups = count // SUB
        top = jnp.zeros((SUB, LC), F32)
        for j in range(2):
            v = cbuf[index(j)].reshape(groups, SUB, LC)
            top = jnp.maximum(top, jnp.max(jnp.abs(v), axis=0))
        power = jnp.minimum(jnp.maximum(jnp.ceil(jnp.log2(top)), -100.0), 100.0)
        factor = jnp.exp2(-power) * LEVELS
        for j in range(2):
            v = cbuf[index(j)].reshape(groups, SUB, LC) * factor[None]
            whole = jnp.round(v).astype(jnp.int32).astype(I16)
            dst[pl.ds(j * count, count), :] = whole.reshape(count, LC)
        power = power.astype(jnp.int32)
        dst[pl.ds(2 * count, 16), :] = jnp.concatenate([power, power], axis=0).astype(I16)

    def scale_of(src, count):
        power = src[pl.ds(2 * count, 16), :].astype(jnp.int32).astype(F32)[:SUB]
        return jnp.exp2(power) * (1.0 / LEVELS)

    def unpack(src, scale, j, count):
        v = src[pl.ds(j * count, count), :].astype(jnp.int32).astype(F32)
        return v.reshape(count // SUB, SUB, LC) * scale[None]

    RING = HALF * 2 * 16
    MATE = HALF * 16

    def arm(n, way):
        return jnp.where(lax.rem(n, 2) == way, LONG, SHORT)

    def hop(n, way, k):
        step = 1 if way == 0 else Z - 1
        where = at_chip(p, yh, lax.rem(z + step, Z))
        slot = jnp.where(lax.rem(n, 2) == way, k, LONG + k)
        return copy(sbuf.at[n, slot], rbuf.at[n, slot], r_s.at[0], r_r.at[n, slot], where)

    def multiply(n, depth):
        product = jnp.dot(
            mfull[:, :, depth].reshape(RING, 2 * CT * TILE), lbuf[n].reshape(2 * CT * TILE, WP),
            preferred_element_type=F32)
        cbuf[n, :, :, depth] = product.reshape(HALF, 2, 16, WP)

    def ring_step(n, way, k):
        length = arm(n, way)
        left = length - k
        depth = lax.rem(z + Z + (left if way == 0 else -left), Z)

        @pl.when(k < length)
        def _():
            multiply(n, depth)

        @pl.when(jnp.logical_and(k > 0, k <= length))
        def _():
            hop(n, way, k - 1).wait_recv()
            src = rbuf.at[n, jnp.where(lax.rem(n, 2) == way, k - 1, LONG + k - 1)]
            scale = scale_of(src, RING)
            for j in range(2):
                index = piece(n, depth, j)
                shape = (HALF, 2, 16, LC)
                cbuf[index] = cbuf[index] + unpack(src, scale, j, RING).reshape(shape)

        @pl.when(k < length)
        def _():
            slot = jnp.where(lax.rem(n, 2) == way, k, LONG + k)
            pack(lambda j: piece(n, depth, j), sbuf.at[n, slot], RING)
            hop(n, way, k).start()

    def y_copy(n):
        return copy(ysb.at[n], yrb.at[n], y_s.at[0], y_r.at[n], y_mate)

    def c_copy(n):
        return copy(colp.at[n, core], colp.at[n, core], c_s.at[0], c_r.at[n], sibling)

    def arrive(n):
        for step in CLOSE + FAR:
            a2_wait(n, step)
            a3(n, step).start()

        @pl.when(n + AHEAD < COUNT)
        def _():
            spread(n + AHEAD)

        copy(l_bytes(n, NP), l_bytes(n, NP), l_s.at[0], a3_r.at[n], sibling).wait_recv()

        @pl.when(n == 0)
        def _():
            for b in range(CT):
                m_local(b).wait()
            other = mfull.at[:, :, :, :, pl.ds(0, CT * TILE)]
            copy(other, other, m_s.at[0], m_r.at[0], sibling).wait_recv()

    def y_arrive(n):
        y_copy(n).wait_recv()
        src = yrb.at[n]
        scale = scale_of(src, MATE)
        for j in range(2):
            total = cbuf[y_piece(n, yh, j)] + unpack(src, scale, j, MATE).reshape(HALF, 16, LC)
            for a in range(HALF):
                image = -total[a] * keep(n // PARTS, core * HALF + a)
                colp[n, core, a, :, pl.ds(j * LC, LC)] = image.astype(BF16)
        c_copy(n).start()

    def d_copy(n, step):
        other = lax.rem(p // 2 + step, X)
        return copy(dsend.at[n, other], drecv.at[n, step], d_s.at[0], d_r.at[n], x_line(step))

    def f_copy(n, step):
        other = lax.rem(u_me + step, NU)
        return copy(fsend.at[n, other], frecv.at[n, step], f_s.at[0], f_r.at[n], y_line(step))

    def part_lanes(n):
        return pl.ds(pl.multiple_of(lax.rem(n, PARTS) * WP, WP), WP)

    def c_arrive(n):
        c_copy(n).wait_recv()
        dsend[n] = jnp.dot(
            mpt[n // PARTS], colp[n].reshape(RT * 16, WP), preferred_element_type=F32
        ).reshape(X, NU, 2 * Z, WP)
        for step in range(1, X):
            d_copy(n, step).start()

        both = colp[n].reshape(RT, 16, WP).astype(F32)
        picked = jnp.where(core == 0, both[:, :SUB], both[:, SUB:])
        col_ref[n // PARTS, :, :, part_lanes(n)] = picked.astype(BF16)

    def d_arrive(n):
        total = dsend[n, p // 2]
        if X > 1:
            got = drecv.at[n, pl.ds(1, X - 1)]
            copy(got, got, d_s.at[0], d_r.at[n], sibling).wait_recv()
            for step in range(1, X):
                total = total + drecv[n, step]
        fsend[n] = total
        for step in range(1, NU):
            f_copy(n, step).start()

    def f_arrive(n):
        got = frecv.at[n, pl.ds(1, NU - 1)]
        copy(got, got, f_s.at[0], f_r.at[n], sibling).wait_recv()
        total = fsend[n, u_me]
        for step in range(1, NU):
            total = total + frecv[n, step]
        for depth in range(Z):
            esend[depth, n // PARTS, :, part_lanes(n)] = total[2 * depth : 2 * depth + 2]

    @pl.loop(0, (COUNT - 1) * LAG + LONG + 5)
    def _(t):
        @pl.loop(0, COUNT)
        def _(n):
            k = t - n * LAG

            @pl.when(jnp.logical_and(k >= 1, k <= LONG))
            def _():
                for way in range(2):
                    ring_step(n, way, k)

            @pl.when(k == LONG)
            def _():
                pack(lambda j: y_piece(n, 1 - yh, j), ysb.at[n], MATE)
                y_copy(n).start()

        @pl.loop(0, COUNT)
        def _(n):
            k = t - n * LAG

            @pl.when(k == LONG + 4)
            def _():
                f_arrive(n)

            @pl.when(k == LONG + 3)
            def _():
                d_arrive(n)

            @pl.when(k == LONG + 2)
            def _():
                c_arrive(n)

            @pl.when(k == LONG + 1)
            def _():
                y_arrive(n)

            @pl.when(k == 0)
            def _():
                arrive(n)
                for way in range(2):
                    ring_step(n, way, k)
                multiply(n, z)

                @pl.when(n == 0)
                def _():
                    for s in range(SETS):
                        transposed(s)

    def e_copy(step):
        other = lax.rem(z + step, Z)
        return copy(esend.at[other], erecv.at[step], e_s.at[0], e_r.at[0], at_chip(p, yh, other))

    @pl.loop(1, Z)
    def _(step):
        e_copy(step).start()

    got = erecv.at[pl.ds(1, Z - 1)]
    copy(got, got, e_s.at[0], e_r.at[0], sibling).wait_recv()
    total = esend[z]
    for step in range(1, Z):
        total = total + erecv[step]
    diag_ref[...] = dinv_ref[...] - total

    def sent(what, sem):
        copy(what, what, sem.at[0], sem.at[0], sibling).wait_send()

    sent(mfull.at[:, :, :, :, pl.ds(0, CT * TILE)], m_s)
    sent(mf, a0_s)
    sent(l_all(2 * NP - TWINS), l_s)
    sent(sbuf, r_s)
    sent(ysb, y_s)
    sent(colp.at[:, 0], c_s)
    if X > 1:
        sent(dsend.at[:, pl.ds(1, X - 1)], d_s)
    sent(fsend.at[:, pl.ds(1, NU - 1)], f_s)
    sent(got, e_s)

    @pl.loop(0, SETS)
    def _(s):
        for h2 in range(2):
            for twin in range(TWINS):
                @pl.when(jnp.logical_not(a1_is_me(h2, twin)))
                def _():
                    a1(s, h2, twin).wait_send()


def body(anc_inverse, panel, tile_mask, diag_inverse):
    n_row = lax.axis_size("prow")
    n_col = lax.axis_size("pcol")
    sets, rt, _, sub, w = panel.shape
    _, tile, ct, _ = anc_inverse.shape
    nz = n_col // 4
    anc = jnp.transpose(anc_inverse, (0, 2, 1, 3)).reshape(rt, ct, 2, nz, 16, tile)
    slim = panel.reshape(sets, rt, sub, w)
    half, nz, nh = rt // 2, n_col // 4, n_col // n_row
    wp, count = w // PARTS, sets * PARTS
    lc = wp // 2
    hops = nz - 1
    message = 2 * half * 2 * 16 + 16
    mate = 2 * half * 16 + 16
    dma = pltpu.SemaphoreType.DMA
    vmem = pl.BlockSpec(memory_space=pltpu.VMEM)
    scratch = [
        pltpu.VMEM((half, 2, nz, 16, 2 * ct * tile), BF16),
        pltpu.VMEM((sets, rt, sub, w), F32),
        pltpu.VMEM((sets, rt, sub, w), F32),
        pltpu.VMEM((sets, PARTS, ct, nh, 16, wp), BF16),
        pltpu.VMEM((count, 2 * ct, tile, wp), BF16),
        pltpu.VMEM((count, half, 2, nz, 16, wp), F32),
        pltpu.VMEM((count, hops, message, lc), I16),
        pltpu.VMEM((count, hops, message, lc), I16),
        pltpu.VMEM((count, mate, lc), I16),
        pltpu.VMEM((count, mate, lc), I16),
        pltpu.VMEM((count, 2, half, 16, wp), BF16),
        pltpu.VMEM((w // 2, w), BF16),
        pltpu.VMEM((sets, w // 2, rt * 16), BF16),
        pltpu.VMEM((count, n_row // 2, 4, 2 * nz, wp), F32),
        pltpu.VMEM((count, n_row // 2, 4, 2 * nz, wp), F32),
        pltpu.VMEM((count, 4, 2 * nz, wp), F32),
        pltpu.VMEM((count, 4, 2 * nz, wp), F32),
        pltpu.VMEM((nz, sets, 2, w), F32),
        pltpu.VMEM((nz, sets, 2, w), F32),
        dma((ct,)), dma((1,)), dma((1,)),
        dma((1,)), dma((sets,)),
        dma((sets, 2, 2)), dma((sets, 2)),
        dma((1,)), dma((count, n_row)), dma((count,)),
        dma((1,)), dma((count, hops)),
        dma((1,)), dma((count,)),
        dma((1,)), dma((count,)),
        dma((1,)), dma((count,)),
        dma((1,)), dma((count,)),
        dma((1,)), dma((1,)),
    ]
    column, diag = pl.pallas_call(
        functools.partial(kernel, n_row, n_col),
        out_shape=(
            jax.ShapeDtypeStruct((sets, rt, sub, w), BF16),
            jax.ShapeDtypeStruct(diag_inverse.shape, F32),
        ),
        in_specs=[
            pl.BlockSpec(memory_space=pltpu.SMEM),
            pl.BlockSpec(memory_space=pl.ANY),
            vmem,
            vmem,
        ],
        out_specs=(vmem, vmem),
        scratch_shapes=scratch,
        compiler_params=pltpu.CompilerParams(
            collective_id=0, has_side_effects=True, vmem_limit_bytes=56 * 1024 * 1024
        ),
        name="selected_inverse",
    )(tile_mask, anc, slim, diag_inverse)
    return column.reshape(panel.shape), diag


def solution(mesh):
    in_specs = (
        P(None, "prow", None, "pcol"),
        P(None, None, "prow", "pcol", None),
        P(),
        P(None, ("prow", "pcol"), None),
    )
    out_specs = (P(None, None, "prow", "pcol", None), P(None, ("prow", "pcol"), None))
    return jax.shard_map(body, mesh=mesh, in_specs=in_specs, out_specs=out_specs, check_vma=False)
```

```python
import functools

import jax
import jax.numpy as jnp
from jax import lax
from jax.experimental import pallas as pl
from jax.experimental.pallas import tpu as pltpu
from jax.sharding import PartitionSpec as P

MESH = pl.DeviceIdType.MESH
F32 = jnp.float32
BF16 = jnp.bfloat16
I16 = jnp.int16
SUB = 8
LEVELS = 32000.0
PARTS = 2
LAG = 1
AHEAD = 2


def kernel(
    NP, NCOL, mask_ref, anc_ref, panel_ref, dinv_ref, col_ref, diag_ref,
    mfull, mf, sib, mpair, lbuf, cbuf, sbuf, rbuf, ysb, yrb, colp, perm, mpt,
    dsend, drecv, fsend, frecv, esend, erecv,
    m_l, m_s, m_r, a0_s, a0_r, a1_s, a1_r, l_s, a2_r, a3_r,
    r_s, r_r, y_s, y_r, c_s, c_r, d_s, d_r, f_s, f_r, e_s, e_r,
):
    SETS, RT, _, W = panel_ref.shape
    CT = anc_ref.shape[1]
    TILE = anc_ref.shape[-1]
    HALF = RT // 2
    NC = NCOL // 2
    Z = NC // 2
    NH = NCOL // NP
    WP = W // PARTS
    COUNT = SETS * PARTS
    LC = WP // 2
    WH = W // 2
    X = NP // 2
    NU = 4
    LONG = Z // 2
    SHORT = Z - 1 - LONG

    p = lax.axis_index("prow")
    q = lax.axis_index("pcol")
    core = lax.rem(q, 2)
    chip = q // 2
    z = lax.rem(chip, Z)
    yh = chip // Z
    sibling = (p, q + 1 - 2 * core)

    def at_chip(row, y, depth):
        return (row, (y * Z + depth) * 2 + core)

    u_me = lax.rem(p, 2) * 2 + yh

    def x_line(step):
        return at_chip(2 * lax.rem(p // 2 + step, X) + lax.rem(p, 2), yh, z)

    def y_line(step):
        other = lax.rem(u_me + step, NU)
        return at_chip(2 * (p // 2) + other // 2, lax.rem(other, 2), z)

    y_mate = at_chip(p, 1 - yh, z)
    y_cross = (p, ((1 - yh) * Z + z) * 2 + 1 - core)

    def turn(depth):
        return lax.rem(depth, X) + (X // 2) * (depth // X)

    def held(row, depth, c):
        return c * Z + 2 * lax.rem(row // 2 + 2 * X - turn(depth), X) + lax.rem(row, 2)

    TWINS = 1
    mine = held(p, z, core)
    far = held(2 * lax.rem(p // 2 + X // 2, X) + lax.rem(p, 2), z, core)

    def a1_target(h2, twin):
        depth = h2 * X + p // 2
        row = 2 * lax.rem(z // 2 + turn(depth) + twin * (X // 2), X) + lax.rem(z, 2)
        return (row, (core * Z + depth) * 2 + yh)

    def a1_is_me(h2, twin):
        row, column = a1_target(h2, twin)
        return jnp.logical_and(row == p, column == q)

    def a1_source(half, twin):
        return (2 * lax.rem(z, X) + half, 2 * (far if twin else mine) + yh)

    def signal(where):
        pl.semaphore_signal(barrier, inc=1, device_id=where, device_id_type=MESH)

    barrier = pltpu.get_barrier_semaphore()
    signal(sibling)
    signal(y_cross)

    for step in range(1, X):
        signal(x_line(step))
    for step in range(1, NU):
        signal(y_line(step))
    for step in range(3, NP, 2):
        signal((2 * lax.rem(p // 2 + step // 2, X) + lax.rem(p + 1, 2), q))


    @pl.loop(1, Z)
    def _(step):
        signal(at_chip(p, yh, lax.rem(z + step, Z)))

    expected = 2 + 2 * (X - 1) + (NU - 1) + (Z - 1)
    for twin in range(TWINS):
        for e in range(2):
            me = a1_is_me(e, twin)
            row, column = a1_source(e, twin)
            from_me = jnp.logical_and(row == p, column == q)

            @pl.when(jnp.logical_not(me))
            def _():
                signal(a1_target(e, twin))

            @pl.when(jnp.logical_not(from_me))
            def _():
                signal((row, column))

            expected = expected + jnp.where(me, 0, 1) + jnp.where(from_me, 0, 1)

    def copy(src, dst, send, recv, where):
        return pltpu.make_async_remote_copy(
            src_ref=src, dst_ref=dst, send_sem=send, recv_sem=recv,
            device_id=where, device_id_type=MESH,
        )

    def lanes(half, b):
        return pl.ds(pl.multiple_of((half * CT + b) * TILE, TILE), TILE)

    def m_local(b):
        return pltpu.make_async_copy(
            anc_ref.at[pl.ds(core * HALF, HALF), b], mfull.at[:, :, :, :, lanes(core, b)], m_l.at[b])

    def m_swap(b):
        return copy(
            anc_ref.at[pl.ds((1 - core) * HALF, HALF), b], mfull.at[:, :, :, :, lanes(core, b)],
            m_s.at[0], m_r.at[0], sibling)

    for b in range(CT):
        m_local(b).start()

    def keep(s, a):
        return mask_ref[s, a * NP + p].astype(F32)

    @pl.loop(0, SETS)
    def _(s):
        @pl.loop(0, RT)
        def _(a):
            mf[s, a] = panel_ref[s, a].astype(F32) * keep(s, a)

    rows = lax.broadcasted_iota(jnp.int32, (WH, W), 0)
    columns = lax.broadcasted_iota(jnp.int32, (WH, W), 1)
    hit = columns == (rows >> 1) * 4 + 2 * core + (rows & 1)
    perm[...] = jnp.where(hit, 1.0, 0.0).astype(BF16)

    pl.semaphore_wait(barrier, expected)

    def a0(s):
        return copy(mf.at[s], sib.at[s], a0_s.at[0], a0_r.at[s], sibling)

    for s in range(SETS):
        a0(s).start()

    def l_slice(n, index):
        return lbuf.at[n, :, pl.ds(pl.multiple_of(16 * index, 16), 16), :]

    def l_bytes(n, count):
        return lbuf.at[n, :, pl.ds(0, 16 * count), :]

    def l_all(count):
        return lbuf.at[:, :, pl.ds(0, 16 * count), :]

    def a1_dst(s):
        return lbuf.at[
            pl.ds(s * PARTS, PARTS), pl.ds(lax.rem(p, 2) * CT, CT),
            pl.ds(pl.multiple_of(16 * chip, 16), 16), :]

    def a1(s, h2, twin):
        return copy(
            mpair.at[s, :, :, 2 * core + h2], a1_dst(s), a1_s.at[s, h2, twin], a1_r.at[s, twin],
            a1_target(h2, twin))

    def a1_local(s, h2, twin):
        return pltpu.make_async_copy(mpair.at[s, :, :, 2 * core + h2], a1_dst(s), a1_r.at[s, twin])

    def a1_wait(s, twin):
        index = far if twin else mine
        got = lbuf.at[pl.ds(s * PARTS, PARTS), :, pl.ds(pl.multiple_of(16 * index, 16), 16), :]
        copy(got, got, a1_s.at[s, 0, twin], a1_r.at[s, twin], sibling).wait_recv()

    @pl.loop(0, SETS)
    def _(s):
        a0(s).wait_recv()
        own = mf[s]
        other = sib[s]
        low = jnp.where(core == 0, own, other)
        high = jnp.where(core == 0, other, own)
        both = jnp.concatenate([low, high], axis=1).astype(BF16).reshape(CT, NH, 16, W)
        for w in range(PARTS):
            mpair[s, w] = both[..., w * WP : (w + 1) * WP]
        for twin in range(TWINS):
            for h2 in range(2):
                me = a1_is_me(h2, twin)

                @pl.when(me)
                def _():
                    a1_local(s, h2, twin).start()

                @pl.when(jnp.logical_not(me))
                def _():
                    a1(s, h2, twin).start()

    def transposed(s):
        total = jnp.zeros((WH, RT * 16), F32)
        for w in range(PARTS):
            total = total + lax.dot_general(
                perm[:, w * WP : (w + 1) * WP], mpair[s, w].reshape(RT * 16, WP),
                (((1,), (1,)), ((), ())), preferred_element_type=F32)
        mpt[s] = total.astype(BF16)

    def across(step):
        return (2 * lax.rem(p // 2 + step // 2, X) + lax.rem(p + step, 2), q)

    def origin(step):
        row = lax.rem(p // 2 + X - step // 2, X)
        return held(2 * row + lax.rem(p + step, 2), z, core)

    def a2(n, step):
        return copy(l_slice(n, mine), l_slice(n, mine), l_s.at[0], a2_r.at[n, step], across(step))

    def a2_wait(n, step):
        copy(l_slice(n, mine), l_slice(n, mine), l_s.at[0], a2_r.at[n, step], sibling).wait_recv()

    def a2_sibling(n):
        return copy(l_slice(n, mine), l_slice(n, mine), l_s.at[0], a3_r.at[n], sibling)

    def a3(n, step):
        index = origin(step)
        return copy(l_slice(n, index), l_slice(n, index), l_s.at[0], a3_r.at[n], sibling)

    FAR = [step for step in range(1, NP) if X > 1 and step // 2 == X // 2]
    CLOSE = [step for step in range(1, NP) if step not in FAR]

    def spread(n):
        @pl.when(lax.rem(n, PARTS) == 0)
        def _():
            a1_wait(n // PARTS, 0)

        for step in FAR + CLOSE[1:] + CLOSE[:1]:
            a2(n, step).start()

        a2_sibling(n).start()

    for b in range(CT):
        m_swap(b).start()

    @pl.loop(0, AHEAD)
    def _(n):
        spread(n)

    def piece(n, depth, j):
        return (n, slice(None), slice(None), depth, slice(None), pl.ds(j * LC, LC))

    def y_piece(n, y, j):
        return (n, slice(None), y, z, slice(None), pl.ds(j * LC, LC))

    def pack(index, dst, count):
        groups = count // SUB
        top = jnp.zeros((SUB, LC), F32)
        for j in range(2):
            v = cbuf[index(j)].reshape(groups, SUB, LC)
            top = jnp.maximum(top, jnp.max(jnp.abs(v), axis=0))
        power = jnp.minimum(jnp.maximum(jnp.ceil(jnp.log2(top)), -100.0), 100.0)
        factor = jnp.exp2(-power) * LEVELS
        for j in range(2):
            v = cbuf[index(j)].reshape(groups, SUB, LC) * factor[None]
            whole = jnp.round(v).astype(jnp.int32).astype(I16)
            dst[pl.ds(j * count, count), :] = whole.reshape(count, LC)
        power = power.astype(jnp.int32)
        dst[pl.ds(2 * count, 16), :] = jnp.concatenate([power, power], axis=0).astype(I16)

    def scale_of(src, count):
        power = src[pl.ds(2 * count, 16), :].astype(jnp.int32).astype(F32)[:SUB]
        return jnp.exp2(power) * (1.0 / LEVELS)

    def unpack(src, scale, j, count):
        v = src[pl.ds(j * count, count), :].astype(jnp.int32).astype(F32)
        return v.reshape(count // SUB, SUB, LC) * scale[None]

    RING = HALF * 2 * 16
    MATE = HALF * 16

    def arm(n, way):
        return jnp.where(lax.rem(n, 2) == way, LONG, SHORT)

    def hop(n, way, k):
        step = 1 if way == 0 else Z - 1
        where = at_chip(p, yh, lax.rem(z + step, Z))
        slot = jnp.where(lax.rem(n, 2) == way, k, LONG + k)
        return copy(sbuf.at[n, slot], rbuf.at[n, slot], r_s.at[0], r_r.at[n, slot], where)

    def multiply(n, depth):
        product = jnp.dot(
            mfull[:, :, depth].reshape(RING, 2 * CT * TILE), lbuf[n].reshape(2 * CT * TILE, WP),
            preferred_element_type=F32)
        cbuf[n, :, :, depth] = product.reshape(HALF, 2, 16, WP)

    def ring_step(n, way, k):
        length = arm(n, way)
        left = length - k
        depth = lax.rem(z + Z + (left if way == 0 else -left), Z)

        @pl.when(k < length)
        def _():
            multiply(n, depth)

        @pl.when(jnp.logical_and(k > 0, k <= length))
        def _():
            hop(n, way, k - 1).wait_recv()
            src = rbuf.at[n, jnp.where(lax.rem(n, 2) == way, k - 1, LONG + k - 1)]
            scale = scale_of(src, RING)
            for j in range(2):
                index = piece(n, depth, j)
                shape = (HALF, 2, 16, LC)
                cbuf[index] = cbuf[index] + unpack(src, scale, j, RING).reshape(shape)

        @pl.when(k < length)
        def _():
            slot = jnp.where(lax.rem(n, 2) == way, k, LONG + k)
            pack(lambda j: piece(n, depth, j), sbuf.at[n, slot], RING)
            hop(n, way, k).start()

    def y_copy(n, cross):
        return copy(
            ysb.at[n, 0], yrb.at[n, cross], y_s.at[cross], y_r.at[n, cross],
            y_cross if cross else y_mate)

    def c_copy(n):
        return copy(ysb.at[n, 1], yrb.at[n, 2], c_s.at[0], c_r.at[n], sibling)

    def arrive(n):
        for step in CLOSE + FAR:
            a2_wait(n, step)
            a3(n, step).start()

        @pl.when(n + AHEAD < COUNT)
        def _():
            spread(n + AHEAD)

        copy(l_bytes(n, NP), l_bytes(n, NP), l_s.at[0], a3_r.at[n], sibling).wait_recv()

        @pl.when(n == 0)
        def _():
            for b in range(CT):
                m_local(b).wait()
            other = mfull.at[:, :, :, :, pl.ds(0, CT * TILE)]
            copy(other, other, m_s.at[0], m_r.at[0], sibling).wait_recv()

    def y_arrive(n):
        c_copy(n).wait_recv()
        for cross in range(2):
            y_copy(n, cross).wait_recv()
        for cross in range(2):
            near = yrb.at[n, 2] if cross else ysb.at[n, 1]
            away = yrb.at[n, cross]
            half = 1 - core if cross else core
            near_scale, away_scale = scale_of(near, MATE), scale_of(away, MATE)
            for j in range(2):
                total = unpack(near, near_scale, j, MATE) + unpack(away, away_scale, j, MATE)
                total = total.reshape(HALF, 16, LC)
                for a in range(HALF):
                    image = -total[a] * keep(n // PARTS, half * HALF + a)
                    colp[n, half, a, :, pl.ds(j * LC, LC)] = image.astype(BF16)

    def d_copy(n, step):
        other = lax.rem(p // 2 + step, X)
        return copy(dsend.at[n, other], drecv.at[n, step], d_s.at[0], d_r.at[n], x_line(step))

    def f_copy(n, step):
        other = lax.rem(u_me + step, NU)
        return copy(fsend.at[n, other], frecv.at[n, step], f_s.at[0], f_r.at[n], y_line(step))

    def part_lanes(n):
        return pl.ds(pl.multiple_of(lax.rem(n, PARTS) * WP, WP), WP)

    def c_arrive(n):
        dsend[n] = jnp.dot(
            mpt[n // PARTS], colp[n].reshape(RT * 16, WP), preferred_element_type=F32
        ).reshape(X, NU, 2 * Z, WP)
        for step in range(1, X):
            d_copy(n, step).start()

        both = colp[n].reshape(RT, 16, WP).astype(F32)
        picked = jnp.where(core == 0, both[:, :SUB], both[:, SUB:])
        col_ref[n // PARTS, :, :, part_lanes(n)] = picked.astype(BF16)

    def d_arrive(n):
        total = dsend[n, p // 2]
        if X > 1:
            got = drecv.at[n, pl.ds(1, X - 1)]
            copy(got, got, d_s.at[0], d_r.at[n], sibling).wait_recv()
            for step in range(1, X):
                total = total + drecv[n, step]
        fsend[n] = total
        for step in range(1, NU):
            f_copy(n, step).start()

    def f_arrive(n):
        got = frecv.at[n, pl.ds(1, NU - 1)]
        copy(got, got, f_s.at[0], f_r.at[n], sibling).wait_recv()
        total = fsend[n, u_me]
        for step in range(1, NU):
            total = total + frecv[n, step]
        for depth in range(Z):
            esend[depth, n // PARTS, :, part_lanes(n)] = total[2 * depth : 2 * depth + 2]

    @pl.loop(0, (COUNT - 1) * LAG + LONG + 4)
    def _(t):
        @pl.loop(0, COUNT)
        def _(n):
            k = t - n * LAG

            @pl.when(jnp.logical_and(k >= 1, k <= LONG))
            def _():
                for way in range(2):
                    ring_step(n, way, k)

            @pl.when(k == LONG)
            def _():
                pack(lambda j: y_piece(n, 1 - yh, j), ysb.at[n, 0], MATE)
                for cross in range(2):
                    y_copy(n, cross).start()
                pack(lambda j: y_piece(n, yh, j), ysb.at[n, 1], MATE)
                c_copy(n).start()

        @pl.loop(0, COUNT)
        def _(n):
            k = t - n * LAG

            @pl.when(k == LONG + 3)
            def _():
                f_arrive(n)

            @pl.when(k == LONG + 2)
            def _():
                d_arrive(n)

            @pl.when(k == LONG + 1)
            def _():
                y_arrive(n)
                c_arrive(n)

            @pl.when(k == 0)
            def _():
                arrive(n)
                for way in range(2):
                    ring_step(n, way, k)
                multiply(n, z)

                @pl.when(n == 0)
                def _():
                    for s in range(SETS):
                        transposed(s)

    def e_copy(step):
        other = lax.rem(z + step, Z)
        return copy(esend.at[other], erecv.at[step], e_s.at[0], e_r.at[0], at_chip(p, yh, other))

    @pl.loop(1, Z)
    def _(step):
        e_copy(step).start()

    got = erecv.at[pl.ds(1, Z - 1)]
    copy(got, got, e_s.at[0], e_r.at[0], sibling).wait_recv()
    total = esend[z]
    for step in range(1, Z):
        total = total + erecv[step]
    diag_ref[...] = dinv_ref[...] - total

    def sent(what, sem):
        copy(what, what, sem.at[0], sem.at[0], sibling).wait_send()

    sent(mfull.at[:, :, :, :, pl.ds(0, CT * TILE)], m_s)
    sent(mf, a0_s)
    sent(l_all(2 * NP - TWINS), l_s)
    sent(sbuf, r_s)
    for cross in range(2):
        copy(ysb.at[:, 0], ysb.at[:, 0], y_s.at[cross], y_s.at[cross], sibling).wait_send()
    sent(ysb.at[:, 1], c_s)
    if X > 1:
        sent(dsend.at[:, pl.ds(1, X - 1)], d_s)
    sent(fsend.at[:, pl.ds(1, NU - 1)], f_s)
    sent(got, e_s)

    @pl.loop(0, SETS)
    def _(s):
        for h2 in range(2):
            for twin in range(TWINS):
                @pl.when(jnp.logical_not(a1_is_me(h2, twin)))
                def _():
                    a1(s, h2, twin).wait_send()


def body(anc_inverse, panel, tile_mask, diag_inverse):
    n_row = lax.axis_size("prow")
    n_col = lax.axis_size("pcol")
    sets, rt, _, sub, w = panel.shape
    _, tile, ct, _ = anc_inverse.shape
    nz = n_col // 4
    anc = jnp.transpose(anc_inverse, (0, 2, 1, 3)).reshape(rt, ct, 2, nz, 16, tile)
    slim = panel.reshape(sets, rt, sub, w)
    half, nz, nh = rt // 2, n_col // 4, n_col // n_row
    wp, count = w // PARTS, sets * PARTS
    lc = wp // 2
    hops = nz - 1
    message = 2 * half * 2 * 16 + 16
    mate = 2 * half * 16 + 16
    dma = pltpu.SemaphoreType.DMA
    vmem = pl.BlockSpec(memory_space=pltpu.VMEM)
    scratch = [
        pltpu.VMEM((half, 2, nz, 16, 2 * ct * tile), BF16),
        pltpu.VMEM((sets, rt, sub, w), F32),
        pltpu.VMEM((sets, rt, sub, w), F32),
        pltpu.VMEM((sets, PARTS, ct, nh, 16, wp), BF16),
        pltpu.VMEM((count, 2 * ct, tile, wp), BF16),
        pltpu.VMEM((count, half, 2, nz, 16, wp), F32),
        pltpu.VMEM((count, hops, message, lc), I16),
        pltpu.VMEM((count, hops, message, lc), I16),
        pltpu.VMEM((count, 2, mate, lc), I16),
        pltpu.VMEM((count, 3, mate, lc), I16),
        pltpu.VMEM((count, 2, half, 16, wp), BF16),
        pltpu.VMEM((w // 2, w), BF16),
        pltpu.VMEM((sets, w // 2, rt * 16), BF16),
        pltpu.VMEM((count, n_row // 2, 4, 2 * nz, wp), F32),
        pltpu.VMEM((count, n_row // 2, 4, 2 * nz, wp), F32),
        pltpu.VMEM((count, 4, 2 * nz, wp), F32),
        pltpu.VMEM((count, 4, 2 * nz, wp), F32),
        pltpu.VMEM((nz, sets, 2, w), F32),
        pltpu.VMEM((nz, sets, 2, w), F32),
        dma((ct,)), dma((1,)), dma((1,)),
        dma((1,)), dma((sets,)),
        dma((sets, 2, 2)), dma((sets, 2)),
        dma((1,)), dma((count, n_row)), dma((count,)),
        dma((1,)), dma((count, hops)),
        dma((2,)), dma((count, 2)),
        dma((1,)), dma((count,)),
        dma((1,)), dma((count,)),
        dma((1,)), dma((count,)),
        dma((1,)), dma((1,)),
    ]
    column, diag = pl.pallas_call(
        functools.partial(kernel, n_row, n_col),
        out_shape=(
            jax.ShapeDtypeStruct((sets, rt, sub, w), BF16),
            jax.ShapeDtypeStruct(diag_inverse.shape, F32),
        ),
        in_specs=[
            pl.BlockSpec(memory_space=pltpu.SMEM),
            pl.BlockSpec(memory_space=pl.ANY),
            vmem,
            vmem,
        ],
        out_specs=(vmem, vmem),
        scratch_shapes=scratch,
        compiler_params=pltpu.CompilerParams(
            collective_id=0, has_side_effects=True, vmem_limit_bytes=56 * 1024 * 1024
        ),
        name="selected_inverse",
    )(tile_mask, anc, slim, diag_inverse)
    return column.reshape(panel.shape), diag


def solution(mesh):
    in_specs = (
        P(None, "prow", None, "pcol"),
        P(None, None, "prow", "pcol", None),
        P(),
        P(None, ("prow", "pcol"), None),
    )
    out_specs = (P(None, None, "prow", "pcol", None), P(None, ("prow", "pcol"), None))
    return jax.shard_map(body, mesh=mesh, in_specs=in_specs, out_specs=out_specs, check_vma=False)
```
